128 devices in a mesh: rep: 4 (over y_lo, core), fsdp: 32 (over z, x, y_hi).
Axes of the slice: x: 4, y: 4 (y_hi: 2, y_lo: 2; y = y_hi * 2 + y_lo), z: 4, core: 2. Of those that a mesh axis runs over, the one named last changes fastest.
Arguments:
- inputs: bfloat16 [4, 12288, 2304], P('rep', 'fsdp'), may hold values from -6 to 6
- cotangent: bfloat16 [4, 12288, 4608], P('rep', 'fsdp'), may hold values from -6 to 6
- params: float32 [4, 2304, 4608], P('rep', 'fsdp'), may hold values from -5 to 5
- first_moment: float32 [4, 2304, 4608], P('rep', 'fsdp'), may hold values from -5 to 5
- second_moment: float32 [4, 2304, 4608], P('rep', 'fsdp'), may hold values from 0.3 to 3
- snapshot: float32 [2304, 1152], P('fsdp'), may hold values from -5 to 5
- momentum: float32 [2304, 1152], P('fsdp'), may hold values from -4 to 4
- fragment: int32 [4], replicated, may hold values from 0 to 3, each once
Outputs:
- new_params: float32 [4, 2304, 4608], P('rep', 'fsdp')
- new_first: float32 [4, 2304, 4608], P('rep', 'fsdp')
- new_second: float32 [4, 2304, 4608], P('rep', 'fsdp')
- input_grad: bfloat16 [4, 12288, 2304], P('rep', 'fsdp')
- new_momentum: float32 [2304, 1152], P('fsdp')
- new_snapshot: float32 [2304, 1152], P('fsdp')
The draws below stay inside these ranges and needn't reach their ends.
Inputs may be any that keep to these rules, and one draw needn't show every extreme that they name: Each fragment appears once; fragment[0] is the fragment whose outer step this window takes.
All inputs are finite; a program needn't handle non-finite values.
Results may differ from the reference program's by a relative error of at most 0.023.
Values may be sent and summed in bfloat16 or wider, within the bound.
A program may use at most 192 MiB of HBM per device.

```python
import math
import jax
import jax.numpy as jnp
from jax import lax

D = 2304
FFW = 4608
FRAGS = 4
TOK_DEV = 384
FRAG = 1152
REPS = 4
TOKENS_R = 12288
N_REP = 4
N_FSDP = 32


def with_spikes(array, stream_key, source, target, parts, factor):
    def block_of(position):
        return (jnp.arange(array.shape[position]) // (array.shape[position] // parts)).reshape((-1,) + (1,) * (array.ndim - 1 - position))

    one_side = jax.random.permutation(stream_key, parts)[block_of(target)]
    far = (block_of(target) + parts // 2) % parts
    return jnp.where((block_of(source) == one_side) | (block_of(source) == far), factor * array, array)


def block_scale(key, dims, split, least, top_value):
    level = 1.0
    for position, shards_of in split:
        steps = jax.random.uniform(jax.random.fold_in(jax.random.fold_in(key, 6), position), (shards_of,), jnp.float32, least / len(split), top_value / len(split))
        level = level * jnp.repeat(jnp.exp(steps), dims[position] // shards_of).reshape((-1,) + (1,) * (len(dims) - 1 - position))
    return level


def gaussian(key, dims, deviation, most, pieces=(), kind=jnp.bfloat16):
    array = jax.random.normal(key, dims, jnp.float32) * deviation
    if len(pieces) > 0:
        array = block_scale(key, dims, pieces, -0.22, 0.18) * array
    return jnp.clip(array, min=-most, max=most).astype(kind)


def heavy_noise(own_key, extent, scale, reach, cuts, heavy, dtype=jnp.bfloat16):
    result = scale * jax.random.normal(own_key, extent, jnp.float32)
    if cuts:
        result = result * block_scale(own_key, extent, cuts, -0.22, 0.18)
    return jnp.clip(with_spikes(result, jax.random.fold_in(own_key, 3), *heavy), -reach, reach).astype(dtype)


def setup_inputs(seed: int = 0) -> dict:
    keys = jax.random.split(jax.random.key(seed), 9)
    inputs = heavy_noise(keys[0], (REPS, TOKENS_R, D), 1.0, 6.0, ((0, 4), (1, 32)), (1, 2, 32, 2.75))
    cotangent = gaussian(keys[1], (REPS, TOKENS_R, FFW), 1.0, 6.0, ((0, 4), (1, 32)))
    params = gaussian(keys[2], (REPS, D, FFW), 1.0, 5.0, ((0, 4), (1, 32)), jnp.float32)
    first_moment = gaussian(keys[3], (REPS, D, FFW), 1.0, 5.0, ((0, 4), (1, 32)), jnp.float32)
    second_moment = jnp.clip(jnp.exp(math.log(3.0) - 2.3025851 * jax.random.uniform(keys[4], (REPS, D, FFW), jnp.float32) ** block_scale(keys[4], (REPS, D, FFW), ((0, 4), (1, 32)), -0.2, 0.2)), 0.3, 3.0)
    snapshot = gaussian(keys[5], (D, FRAG), 1.0, 5.0, ((0, 32),), jnp.float32)
    momentum = gaussian(keys[6], (D, FRAG), 0.5, 4.0, ((0, 32),), jnp.float32)
    fragment = jax.random.permutation(keys[7], FRAGS).astype(jnp.int32)
    return dict(inputs=inputs, cotangent=cotangent, params=params, first_moment=first_moment, second_moment=second_moment, snapshot=snapshot, momentum=momentum, fragment=fragment)


beta_one = 0.9
beta_two = 0.95
inner_rate = 0.01
adam_eps = 1e-08
decay_rate = 0.1
outer_rate = 0.7
outer_mu = 0.9
mix_rate = 0.5

def gelu_cot(pre, cot):
    return jax.vjp(lambda t: jax.nn.gelu(t, approximate=True), pre)[1](cot)[0]

def reference(inputs, cotangent, params, first_moment, second_moment, snapshot, momentum, fragment):
    scale = D ** (-0.5)
    start_col = fragment[0].astype(jnp.int32) * FRAG
    delta_sum = jnp.zeros((D, FRAG), jnp.float32)
    for rep_index in range(N_REP):
        local = lax.dynamic_slice_in_dim(params[rep_index], start_col, FRAG, 1)
        delta_sum = delta_sum + (snapshot - local)
    outer_grad = delta_sum / N_REP
    new_momentum = outer_mu * momentum + outer_grad
    new_snapshot = snapshot - outer_rate * (outer_grad + outer_mu * new_momentum)
    params_out, first_out, second_out, grads_out = ([], [], [], [])
    for rep_index in range(N_REP):
        weights = params[rep_index].astype(jnp.bfloat16)
        acts = inputs[rep_index]
        pre = jnp.dot(acts, weights, preferred_element_type=jnp.float32) * scale
        hidden_cot = (gelu_cot(pre, cotangent[rep_index].astype(jnp.float32)) * scale).astype(jnp.bfloat16)
        back = lax.dot_general(hidden_cot, weights, (((1,), (1,)), ((), ())), preferred_element_type=jnp.float32)
        grads_out.append(back.astype(jnp.bfloat16))
        act_blocks = acts.reshape(N_FSDP, TOK_DEV, D)
        cot_blocks = hidden_cot.reshape(N_FSDP, TOK_DEV, FFW)

        def add_block(total, pair):
            term = lax.dot_general(pair[0], pair[1], (((0,), (0,)), ((), ())), preferred_element_type=jnp.float32)
            term = lax.optimization_barrier(term.astype(jnp.bfloat16))
            return (total + term.astype(jnp.float32), None)
        grad, _ = lax.scan(add_block, jnp.zeros((D, FFW), jnp.float32), (act_blocks, cot_blocks))
        first = beta_one * first_moment[rep_index] + (1.0 - beta_one) * grad
        second = beta_two * second_moment[rep_index] + (1.0 - beta_two) * grad * grad
        old = params[rep_index]
        stepped = old - inner_rate * (first / (jnp.sqrt(second) + adam_eps) + decay_rate * old)
        frag_part = lax.dynamic_slice_in_dim(stepped, start_col, FRAG, 1)
        merged = mix_rate * new_snapshot + (1.0 - mix_rate) * frag_part
        stepped = lax.dynamic_update_slice_in_dim(stepped, merged, start_col, 1)
        params_out.append(stepped)
        first_out.append(first)
        second_out.append(second)
    return (jnp.stack(params_out), jnp.stack(first_out), jnp.stack(second_out), jnp.stack(grads_out), new_momentum, new_snapshot)
```

```python
import functools

import jax
import jax.numpy as jnp
from jax import lax
from jax.experimental import pallas as pl
from jax.experimental.pallas import tpu as pltpu
from jax.sharding import PartitionSpec as P

beta_one = 0.9
beta_two = 0.95
inner_rate = 0.01
adam_eps = 1e-08
decay_rate = 0.1
outer_rate = 0.7
outer_mu = 0.9
mix_rate = 0.5

LANES = 128
CHUNK = 256
MESH = pl.DeviceIdType.MESH
f32 = jnp.float32
bf16 = jnp.bfloat16


def gelu_slope(t):
    c = 0.7978845608028654
    sq = t * t
    th = jnp.tanh(c * t * (1.0 + 0.044715 * sq))
    return 0.5 * (1.0 + th) + 0.5 * t * (1.0 - th * th) * (c * (1.0 + 3 * 0.044715 * sq))


def pair_kernel(
    x_hbm, cot_hbm, p_ref,
    out_ref, g_ref,
    xb, xt, cb, w, g, rah, raf, rbh, rbf, pws, pwr, gps, gpr, bks, bkr, tmp, acc,
    loc_sem, ag_send, ag_recv, rs_send, rs_recv, pw_send, pw_recv,
    x_send, x_recv, cot_send, cot_recv, bk_send, bk_recv, gp_send, gp_recv,
):
    tok, width = x_hbm.shape
    rows, ffw = p_ref.shape
    half_cols = ffw // 2
    n_chunks = half_cols // CHUNK
    block = 2 * rows
    pad_rows = pwr.shape[2]
    cut = (block // 16 + 1) // 2 * 16
    n_x = x_send.shape[0]
    x_rows = tok // n_x
    n_bk = bk_send.shape[0]
    bk_rows = tok // (n_bk // 2)
    bk_cols = width // 2
    scale = width ** (-0.5)

    f = lax.axis_index("fsdp")
    yh = lax.rem(f, 2)
    x = lax.rem(lax.div(f, 2), 4)
    z = lax.div(f, 8)

    def device(zz, xx, yy):
        return {"fsdp": zz * 8 + xx * 2 + yy}

    peer = device(z, x, 1 - yh)
    place = {"x": x, "z": z}
    after = {a: lax.rem(place[a] + 1, 4) for a in place}
    before = {a: lax.rem(place[a] + 3, 4) for a in place}
    across = {a: lax.rem(place[a] + 2, 4) for a in place}
    right = {"x": device(z, after["x"], yh), "z": device(after["z"], x, yh)}
    left = {"x": device(z, before["x"], yh), "z": device(before["z"], x, yh)}
    first_axis = ("x", "z")
    second_axis = ("z", "x")
    my_base = yh * half_cols
    peer_base = (1 - yh) * half_cols

    def seg2(ref, u, p, i):
        return ref.at[u, i] if p == 0 else ref.at[u, :, i]

    def half2(ref, u, p, i, h):
        part = pl.ds(2 * h, 2)
        return ref.at[u, i, part] if p == 0 else ref.at[u, part, i]

    def seg1(ref, u, p, i):
        return ref.at[u, z, i] if p == 0 else ref.at[u, i, x]

    def half1(ref, u, p, i, h):
        part = pl.ds(0, cut) if h == 0 else pl.ds(cut, block - cut)
        return ref.at[u, z, i, part] if p == 0 else ref.at[u, i, x, part]

    def remote(src, dst, send, recv, to):
        return pltpu.make_async_remote_copy(
            src_ref=src, dst_ref=dst, send_sem=send, recv_sem=recv, device_id=to, device_id_type=MESH
        )

    def gather_copy(u, p, k):
        a, b = first_axis[p], second_axis[p]
        part = (
            lambda: seg1(w, u, p, place[a]),
            lambda: seg1(w, u, p, place[a]),
            lambda: half1(w, u, p, before[a], 0),
            lambda: half1(w, u, p, after[a], 1),
            lambda: seg2(w, u, p, place[b]),
            lambda: seg2(w, u, p, place[b]),
            lambda: half2(w, u, p, before[b], 0),
            lambda: half2(w, u, p, after[b], 1),
        )[k]()
        to = (right if k % 2 == 0 else left)[a if k < 4 else b]
        return remote(part, part, ag_send.at[u, k], ag_recv.at[u, k], to)

    def scatter_copy(u, p, k):
        a, b = first_axis[p], second_axis[p]
        src, dst = (
            lambda: (half2(g, u, p, across[b], 0), rah.at[u, 0]),
            lambda: (half2(g, u, p, across[b], 1), rah.at[u, 1]),
            lambda: (seg2(g, u, p, after[b]), raf.at[u, 0]),
            lambda: (seg2(g, u, p, before[b]), raf.at[u, 1]),
            lambda: (half1(g, u, p, across[a], 0), rbh.at[u, pl.ds(0, cut)]),
            lambda: (half1(g, u, p, across[a], 1), rbh.at[u, pl.ds(cut, block - cut)]),
            lambda: (seg1(g, u, p, after[a]), rbf.at[u, 0]),
            lambda: (seg1(g, u, p, before[a]), rbf.at[u, 1]),
        )[k]()
        to = (right if k % 2 == 0 else left)[b if k < 4 else a]
        return remote(src, dst, rs_send.at[u, k], rs_recv.at[u, k], to)

    def pw_copy(c):
        return remote(pws.at[c], pwr.at[c], pw_send.at[c], pw_recv.at[c], peer)

    def x_copy(i):
        return remote(
            x_hbm.at[pl.ds(i * x_rows, x_rows)], xb.at[pl.ds(tok + i * x_rows, x_rows)],
            x_send.at[i], x_recv.at[i], peer,
        )

    def cot_copy(c):
        cols = pl.ds(pl.multiple_of(peer_base + c * CHUNK, CHUNK), CHUNK)
        return remote(
            cot_hbm.at[:, cols], cb.at[c, pl.ds(tok, tok)], cot_send.at[c], cot_recv.at[c], peer
        )

    def bk_copy(i):
        return remote(bks.at[i], bkr.at[i], bk_send.at[i], bk_recv.at[i], peer)

    def gp_copy(u):
        return remote(gps.at[u], gpr.at[u], gp_send.at[u], gp_recv.at[u], peer)

    def own_x():
        return pltpu.make_async_copy(x_hbm, xb.at[pl.ds(0, tok)], loc_sem.at[n_chunks])

    def own_cot(c):
        cols = pl.ds(pl.multiple_of(my_base + c * CHUNK, CHUNK), CHUNK)
        return pltpu.make_async_copy(cot_hbm.at[:, cols], cb.at[c, pl.ds(0, tok)], loc_sem.at[c])

    def each(count, step):
        def run(i, carry):
            step(i)
            return carry
        lax.fori_loop(0, count, run, 0)

    def ranged(t, lag, step):
        @pl.when((t >= lag) & (t < lag + n_chunks))
        def _():
            step(t - lag)

    def both(step):
        def run(c):
            for p in range(2):
                step(2 * c + p, p)
        return run

    own_x().start()
    each(n_chunks, lambda c: own_cot(c).start())

    def prepare(c):
        for h in range(2):
            cols = pl.ds(pl.multiple_of(peer_base + c * CHUNK + h * LANES, LANES), LANES)
            part = jnp.concatenate([p_ref[:, cols], jnp.zeros((pad_rows - rows, LANES), f32)], axis=0)
            pws[c, h] = part.astype(bf16)

    each(n_chunks, prepare)

    barrier = pltpu.get_barrier_semaphore()
    partners = (peer, right["x"], left["x"], right["z"], left["z"])
    for partner in partners:
        pl.semaphore_signal(barrier, inc=1, device_id=partner, device_id_type=MESH)
    pl.semaphore_wait(barrier, len(partners))

    each(n_chunks, lambda c: pw_copy(c).start())
    each(n_x, lambda i: x_copy(i).start())

    def transpose_rows(start, count):
        def step(k):
            cols = pl.ds(pl.multiple_of(k * LANES, LANES), LANES)
            part = xb[pl.ds(start, count), cols].astype(f32)
            xt[cols, pl.ds(start, count)] = part.T.astype(bf16)
        each(width // LANES, step)

    def chunk_weights(c):
        return jnp.concatenate(
            [w[2 * c].reshape(width, LANES), w[2 * c + 1].reshape(width, LANES)], axis=1
        )

    def hidden(c, start):
        at = pl.ds(start, tok)
        pre = jnp.dot(xb[at, :], chunk_weights(c), preferred_element_type=f32) * scale
        cot = cb[c, at, :].astype(f32)
        cb[c, at, :] = (gelu_slope(pre) * cot * scale).astype(bf16)

    def gather_own(c):
        pw_copy(c).wait_recv()
        for h in range(2):
            cols = pl.ds(pl.multiple_of(my_base + c * CHUNK + h * LANES, LANES), LANES)
            tmp[pl.ds(pl.multiple_of(yh * rows, 8), rows), :] = p_ref[:, cols]
            tmp[pl.ds(pl.multiple_of((1 - yh) * rows, 8), rows), :] = pwr[c, h].astype(f32)[:rows]
            w[2 * c + h, z, x] = tmp[...].astype(bf16)
            gather_copy(2 * c + h, h, 0).start()
            gather_copy(2 * c + h, h, 1).start()

    def gather_forward(k):
        def step(u, p):
            gather_copy(u, p, k).wait_recv()
            gather_copy(u, p, k + 2).start()
            gather_copy(u, p, k + 1).wait_recv()
            gather_copy(u, p, k + 3).start()
        return both(step)

    @both
    def gather_second(u, p):
        gather_copy(u, p, 2).wait_recv()
        gather_copy(u, p, 3).wait_recv()
        gather_copy(u, p, 4).start()
        gather_copy(u, p, 5).start()

    @both
    def gather_end(u, p):
        gather_copy(u, p, 6).wait_recv()
        gather_copy(u, p, 7).wait_recv()

    def own_hidden(c):
        gather_end(c)
        own_cot(c).wait()
        hidden(c, 0)

    def gather_tick(t):
        ranged(t, 0, gather_own)
        ranged(t, 1, gather_forward(0))
        ranged(t, 2, gather_second)
        ranged(t, 3, gather_forward(4))

        @pl.when(t == 2)
        def _():
            own_x().wait()
            transpose_rows(0, tok)

        @pl.when(t == n_chunks)
        def _():
            cot_copy(0).start()
            cot_copy(1).start()

        ranged(t, 4, own_hidden)

    each(n_chunks + 4, gather_tick)

    for i in range(n_x):
        x_copy(i).wait_recv()
        transpose_rows(tok + i * x_rows, x_rows)

    def add_into(ref, other):
        ref[...] = (ref[...].astype(f32) + other[...].astype(f32)).astype(bf16)

    def work(c):
        cot_copy(c).wait_recv()

        @pl.when(c + 2 < n_chunks)
        def _():
            cot_copy(c + 2).start()

        hidden(c, tok)

        def block_grad(i):
            at = pl.ds(pl.multiple_of(i * 4 * block, LANES // 2), 4 * block)
            term = jnp.dot(xt[at, :], cb[c], preferred_element_type=f32).astype(bf16)
            g[2 * c, i] = term[:, :LANES].reshape(4, block, LANES)
            g[2 * c + 1, i] = term[:, LANES:].reshape(4, block, LANES)

        each(4, block_grad)
        for p in range(2):
            scatter_copy(2 * c + p, p, 0).start()
            scatter_copy(2 * c + p, p, 1).start()

    @both
    def scatter_second(u, p):
        b = second_axis[p]
        scatter_copy(u, p, 0).wait_recv()
        add_into(half2(g, u, p, after[b], 0), rah.at[u, 0])
        scatter_copy(u, p, 2).start()
        scatter_copy(u, p, 1).wait_recv()
        add_into(half2(g, u, p, before[b], 1), rah.at[u, 1])
        scatter_copy(u, p, 3).start()

    @both
    def scatter_third(u, p):
        b = second_axis[p]
        scatter_copy(u, p, 2).wait_recv()
        scatter_copy(u, p, 3).wait_recv()
        mine = seg2(g, u, p, place[b])
        mine[...] = (
            mine[...].astype(f32) + raf[u, 0].astype(f32) + raf[u, 1].astype(f32)
        ).astype(bf16)
        scatter_copy(u, p, 4).start()
        scatter_copy(u, p, 5).start()

    @both
    def scatter_fourth(u, p):
        a = first_axis[p]
        scatter_copy(u, p, 4).wait_recv()
        add_into(half1(g, u, p, after[a], 0), rbh.at[u, pl.ds(0, cut)])
        scatter_copy(u, p, 6).start()
        scatter_copy(u, p, 5).wait_recv()
        add_into(half1(g, u, p, before[a], 1), rbh.at[u, pl.ds(cut, block - cut)])
        scatter_copy(u, p, 7).start()

    @both
    def scatter_end(u, p):
        a = first_axis[p]
        scatter_copy(u, p, 6).wait_recv()
        scatter_copy(u, p, 7).wait_recv()
        mine = seg1(g, u, p, place[a])
        tmp[...] = mine[...].astype(f32) + rbf[u, 0].astype(f32) + rbf[u, 1].astype(f32)
        theirs = tmp[pl.ds(pl.multiple_of((1 - yh) * rows, 8), rows), :]
        theirs = jnp.concatenate([theirs, jnp.zeros((pad_rows - rows, LANES), f32)], axis=0)
        gps[u] = theirs.astype(bf16)
        gp_copy(u).start()
        cols = pl.ds(pl.multiple_of(my_base + u * LANES, LANES), LANES)
        g_ref[:, cols] = tmp[pl.ds(pl.multiple_of(yh * rows, 8), rows), :]

    def back_tile(i, start):
        m, n = lax.div(i, 2), lax.rem(i, 2)
        at = pl.ds(pl.multiple_of(start + m * bk_rows, 16), bk_rows)
        acc[...] = jnp.zeros_like(acc)

        def step(c):
            part = jnp.concatenate(
                [w[2 * c + h, pl.ds(2 * n, 2)].reshape(bk_cols, LANES) for h in range(2)], axis=1
            )
            acc[...] += lax.dot_general(
                cb[c, at, :], part, (((1,), (1,)), ((), ())), preferred_element_type=f32
            )

        each(n_chunks, step)

    def send_back(i):
        back_tile(i, tok)
        bks[i] = acc[...].astype(bf16)
        bk_copy(i).start()

    def work_tick(t):
        ranged(t, 0, work)

        @pl.when((t >= n_chunks) & (t < n_chunks + n_bk // 2))
        def _():
            send_back(2 * (t - n_chunks))
            send_back(2 * (t - n_chunks) + 1)

        ranged(t, 2, scatter_second)
        ranged(t, 3, scatter_third)
        ranged(t, 4, scatter_fourth)
        ranged(t, 5, scatter_end)

    each(n_chunks + 5, work_tick)

    def finish_back(i):
        back_tile(i, 0)
        bk_copy(i).wait_recv()
        m, n = lax.div(i, 2), lax.rem(i, 2)
        at = pl.ds(pl.multiple_of(m * bk_rows, 16), bk_rows)
        cols = pl.ds(pl.multiple_of(n * bk_cols, LANES), bk_cols)
        out_ref[at, cols] = (acc[...] + bkr[i].astype(f32)).astype(bf16)

    each(n_bk, finish_back)

    def finish_grad(u):
        gp_copy(u).wait_recv()
        cols = pl.ds(pl.multiple_of(peer_base + u * LANES, LANES), LANES)
        g_ref[:, cols] = gpr[u].astype(f32)[:rows]

    each(2 * n_chunks, finish_grad)

    def settle(c):
        pw_copy(c).wait_send()
        cot_copy(c).wait_send()
        for p in range(2):
            u = 2 * c + p
            gp_copy(u).wait_send()
            for k in range(8):
                gather_copy(u, p, k).wait_send()
                scatter_copy(u, p, k).wait_send()

    each(n_chunks, settle)
    each(n_x, lambda i: x_copy(i).wait_send())
    each(n_bk, lambda i: bk_copy(i).wait_send())


def projection(acts, cot, weights):
    tok, width = acts.shape
    rows, ffw = weights.shape
    units = ffw // 2 // LANES
    chunks = units // 2
    block = 2 * rows
    pad_rows = (rows + 15) // 16 * 16
    n_x, n_bk = 3, 6
    dma = pltpu.SemaphoreType.DMA
    vmem = pltpu.VMEM
    return pl.pallas_call(
        pair_kernel,
        out_shape=(
            jax.ShapeDtypeStruct((tok, width), bf16),
            jax.ShapeDtypeStruct((rows, ffw), f32),
        ),
        in_specs=[
            pl.BlockSpec(memory_space=pl.ANY),
            pl.BlockSpec(memory_space=pl.ANY),
            pl.BlockSpec(memory_space=pltpu.VMEM),
        ],
        out_specs=(
            pl.BlockSpec(memory_space=pltpu.VMEM),
            pl.BlockSpec(memory_space=pltpu.VMEM),
        ),
        scratch_shapes=[
            vmem((2 * tok, width), bf16),
            vmem((width, 2 * tok), bf16),
            vmem((chunks, 2 * tok, CHUNK), bf16),
            vmem((units, 4, 4, block, LANES), bf16),
            vmem((units, 4, 4, block, LANES), bf16),
            vmem((units, 2, 2, block, LANES), bf16),
            vmem((units, 2, 4, block, LANES), bf16),
            vmem((units, block, LANES), bf16),
            vmem((units, 2, block, LANES), bf16),
            vmem((chunks, 2, pad_rows, LANES), bf16),
            vmem((chunks, 2, pad_rows, LANES), bf16),
            vmem((units, pad_rows, LANES), bf16),
            vmem((units, pad_rows, LANES), bf16),
            vmem((n_bk, tok // (n_bk // 2), width // 2), bf16),
            vmem((n_bk, tok // (n_bk // 2), width // 2), bf16),
            vmem((block, LANES), f32),
            vmem((tok // (n_bk // 2), width // 2), f32),
            dma((chunks + 1,)),
            dma((units, 8)), dma((units, 8)),
            dma((units, 8)), dma((units, 8)),
            dma((chunks,)), dma((chunks,)),
            dma((n_x,)), dma((n_x,)),
            dma((chunks,)), dma((chunks,)),
            dma((n_bk,)), dma((n_bk,)),
            dma((units,)), dma((units,)),
        ],
        compiler_params=pltpu.CompilerParams(
            collective_id=1, has_side_effects=True, vmem_limit_bytes=60 * 2**20
        ),
        cost_estimate=pl.CostEstimate(
            flops=6 * tok * width * ffw, bytes_accessed=16 * tok * width, transcendentals=tok * ffw
        ),
        name="pair_projection",
    )(acts, cot, weights)


def body(inputs, cotangent, params, first_moment, second_moment, snapshot, momentum, fragment):
    weights = params[0]
    frag = snapshot.shape[1]
    start_col = fragment[0] * frag
    local = lax.dynamic_slice_in_dim(weights, start_col, frag, 1)
    total = lax.psum((snapshot - local).astype(bf16), "rep").astype(f32)
    input_grad, grad = projection(inputs[0], cotangent[0], weights)
    outer_grad = total / lax.axis_size("rep")
    new_momentum = outer_mu * momentum + outer_grad
    new_snapshot = snapshot - outer_rate * (outer_grad + outer_mu * new_momentum)
    first = beta_one * first_moment[0] + (1.0 - beta_one) * grad
    second = beta_two * second_moment[0] + (1.0 - beta_two) * grad * grad
    stepped = weights - inner_rate * (first / (jnp.sqrt(second) + adam_eps) + decay_rate * weights)
    frag_part = lax.dynamic_slice_in_dim(stepped, start_col, frag, 1)
    merged = mix_rate * new_snapshot + (1.0 - mix_rate) * frag_part
    stepped = lax.dynamic_update_slice_in_dim(stepped, merged, start_col, 1)
    return (stepped[None], first[None], second[None], input_grad[None], new_momentum, new_snapshot)


def solution(mesh):
    return jax.shard_map(
        body,
        mesh=mesh,
        in_specs=(
            P("rep", "fsdp", None),
            P("rep", "fsdp", None),
            P("rep", "fsdp", None),
            P("rep", "fsdp", None),
            P("rep", "fsdp", None),
            P("fsdp", None),
            P("fsdp", None),
            P(),
        ),
        out_specs=(
            P("rep", "fsdp", None),
            P("rep", "fsdp", None),
            P("rep", "fsdp", None),
            P("rep", "fsdp", None),
            P("fsdp", None),
            P("fsdp", None),
        ),
        check_vma=False,
    )
```

```python
import functools

import jax
import jax.numpy as jnp
from jax import lax
from jax.experimental import pallas as pl
from jax.experimental.pallas import tpu as pltpu
from jax.sharding import PartitionSpec as P

beta_one = 0.9
beta_two = 0.95
inner_rate = 0.01
adam_eps = 1e-08
decay_rate = 0.1
outer_rate = 0.7
outer_mu = 0.9
mix_rate = 0.5

LANES = 128
CHUNK = 256
MESH = pl.DeviceIdType.MESH
f32 = jnp.float32
bf16 = jnp.bfloat16


def gelu_slope(t):
    c = 0.7978845608028654
    sq = t * t
    th = jnp.tanh(c * t * (1.0 + 0.044715 * sq))
    return 0.5 * (1.0 + th) + 0.5 * t * (1.0 - th * th) * (c * (1.0 + 3 * 0.044715 * sq))


def pair_kernel(
    x_hbm, cot_hbm, p_ref,
    out_ref, g_ref,
    xb, cb, w, g, rah, raf, rbh, rbf, pws, pwr, gps, gpr, bks, bkr, tmp, acc,
    loc_sem, ag_send, ag_recv, rs_send, rs_recv, pw_send, pw_recv,
    x_send, x_recv, cot_send, cot_recv, bk_send, bk_recv, gp_send, gp_recv,
):
    tok, width = x_hbm.shape
    rows, ffw = p_ref.shape
    half_cols = ffw // 2
    n_chunks = half_cols // CHUNK
    block = 2 * rows
    pad_rows = pwr.shape[2]
    cut = (block // 16 + 1) // 2 * 16
    n_x = x_send.shape[0]
    x_rows = tok // n_x
    n_bk = bk_send.shape[0]
    bk_rows = tok // (n_bk // 2)
    bk_cols = width // 2
    scale = width ** (-0.5)
    ahead = 4
    work_lag = 10
    done = work_lag + n_chunks

    f = lax.axis_index("fsdp")
    yh = lax.rem(f, 2)
    x = lax.rem(lax.div(f, 2), 4)
    z = lax.div(f, 8)

    def device(zz, xx, yy):
        return {"fsdp": zz * 8 + xx * 2 + yy}

    peer = device(z, x, 1 - yh)
    place = {"x": x, "z": z}
    after = {a: lax.rem(place[a] + 1, 4) for a in place}
    before = {a: lax.rem(place[a] + 3, 4) for a in place}
    across = {a: lax.rem(place[a] + 2, 4) for a in place}
    right = {"x": device(z, after["x"], yh), "z": device(after["z"], x, yh)}
    left = {"x": device(z, before["x"], yh), "z": device(before["z"], x, yh)}
    first_axis = ("x", "z")
    second_axis = ("z", "x")
    my_base = yh * half_cols
    peer_base = (1 - yh) * half_cols

    def seg2(ref, u, p, i):
        return ref.at[u, i] if p == 0 else ref.at[u, :, i]

    def half2(ref, u, p, i, h):
        part = pl.ds(2 * h, 2)
        return ref.at[u, i, part] if p == 0 else ref.at[u, part, i]

    def seg1(ref, u, p, i):
        return ref.at[u, z, i] if p == 0 else ref.at[u, i, x]

    def half1(ref, u, p, i, h):
        part = pl.ds(0, cut) if h == 0 else pl.ds(cut, block - cut)
        return ref.at[u, z, i, part] if p == 0 else ref.at[u, i, x, part]

    def chunk_cols(c):
        return pl.ds(pl.multiple_of(c * CHUNK, CHUNK), CHUNK)

    def remote(src, dst, send, recv, to):
        return pltpu.make_async_remote_copy(
            src_ref=src, dst_ref=dst, send_sem=send, recv_sem=recv, device_id=to, device_id_type=MESH
        )

    def gather_copy(u, p, k):
        a, b = first_axis[p], second_axis[p]
        part = (
            lambda: seg1(w, u, p, place[a]),
            lambda: seg1(w, u, p, place[a]),
            lambda: half1(w, u, p, before[a], 0),
            lambda: half1(w, u, p, after[a], 1),
            lambda: seg2(w, u, p, place[b]),
            lambda: seg2(w, u, p, place[b]),
            lambda: half2(w, u, p, before[b], 0),
            lambda: half2(w, u, p, after[b], 1),
        )[k]()
        to = (right if k % 2 == 0 else left)[a if k < 4 else b]
        return remote(part, part, ag_send.at[u, k], ag_recv.at[u, k], to)

    def scatter_copy(u, p, k):
        a, b = first_axis[p], second_axis[p]
        src, dst = (
            lambda: (half2(g, u, p, across[b], 0), rah.at[u, 0]),
            lambda: (half2(g, u, p, across[b], 1), rah.at[u, 1]),
            lambda: (seg2(g, u, p, after[b]), raf.at[u, 0]),
            lambda: (seg2(g, u, p, before[b]), raf.at[u, 1]),
            lambda: (half1(g, u, p, across[a], 0), rbh.at[u, pl.ds(0, cut)]),
            lambda: (half1(g, u, p, across[a], 1), rbh.at[u, pl.ds(cut, block - cut)]),
            lambda: (seg1(g, u, p, after[a]), rbf.at[u, 0]),
            lambda: (seg1(g, u, p, before[a]), rbf.at[u, 1]),
        )[k]()
        to = (right if k % 2 == 0 else left)[b if k < 4 else a]
        return remote(src, dst, rs_send.at[u, k], rs_recv.at[u, k], to)

    def pw_copy(c):
        return remote(pws.at[c], pwr.at[c], pw_send.at[c], pw_recv.at[c], peer)

    def x_copy(i):
        return remote(
            x_hbm.at[pl.ds(i * x_rows, x_rows)], xb.at[pl.ds(tok + i * x_rows, x_rows)],
            x_send.at[i], x_recv.at[i], peer,
        )

    def cot_copy(c):
        cols = pl.ds(pl.multiple_of(peer_base + c * CHUNK, CHUNK), CHUNK)
        return remote(
            cot_hbm.at[:, cols], cb.at[pl.ds(tok, tok), chunk_cols(c)],
            cot_send.at[c], cot_recv.at[c], peer,
        )

    def bk_copy(i):
        return remote(bks.at[i], bkr.at[i], bk_send.at[i], bk_recv.at[i], peer)

    def gp_copy(u):
        return remote(gps.at[u], gpr.at[u], gp_send.at[u], gp_recv.at[u], peer)

    def own_x():
        return pltpu.make_async_copy(x_hbm, xb.at[pl.ds(0, tok)], loc_sem.at[n_chunks])

    def own_cot(c):
        cols = pl.ds(pl.multiple_of(my_base + c * CHUNK, CHUNK), CHUNK)
        return pltpu.make_async_copy(
            cot_hbm.at[:, cols], cb.at[pl.ds(0, tok), chunk_cols(c)], loc_sem.at[c]
        )

    def each(count, step):
        def run(i, carry):
            step(i)
            return carry
        lax.fori_loop(0, count, run, 0)

    def ranged(t, lag, step):
        @pl.when((t >= lag) & (t < lag + n_chunks))
        def _():
            step(t - lag)

    def both(step):
        def run(c):
            for p in range(2):
                step(2 * c + p, p)
        return run

    own_x().start()
    each(n_chunks, lambda c: own_cot(c).start())

    def prepare(c):
        for h in range(2):
            cols = pl.ds(pl.multiple_of(peer_base + c * CHUNK + h * LANES, LANES), LANES)
            part = jnp.concatenate([p_ref[:, cols], jnp.zeros((pad_rows - rows, LANES), f32)], axis=0)
            pws[c, h] = part.astype(bf16)

    each(n_chunks, prepare)

    barrier = pltpu.get_barrier_semaphore()
    partners = (peer, right["x"], left["x"], right["z"], left["z"])
    for partner in partners:
        pl.semaphore_signal(barrier, inc=1, device_id=partner, device_id_type=MESH)
    pl.semaphore_wait(barrier, len(partners))

    each(n_chunks, lambda c: pw_copy(c).start())
    each(n_x, lambda i: x_copy(i).start())

    def chunk_weights(c):
        return jnp.concatenate(
            [w[2 * c].reshape(width, LANES), w[2 * c + 1].reshape(width, LANES)], axis=1
        )

    def hidden(c, start):
        at = pl.ds(start, tok)
        pre = jnp.dot(xb[at, :], chunk_weights(c), preferred_element_type=f32) * scale
        cot = cb[at, chunk_cols(c)].astype(f32)
        cb[at, chunk_cols(c)] = (gelu_slope(pre) * cot * scale).astype(bf16)

    def gather_own(c):
        pw_copy(c).wait_recv()
        for h in range(2):
            cols = pl.ds(pl.multiple_of(my_base + c * CHUNK + h * LANES, LANES), LANES)
            tmp[pl.ds(pl.multiple_of(yh * rows, 8), rows), :] = p_ref[:, cols]
            tmp[pl.ds(pl.multiple_of((1 - yh) * rows, 8), rows), :] = pwr[c, h].astype(f32)[:rows]
            w[2 * c + h, z, x] = tmp[...].astype(bf16)
            gather_copy(2 * c + h, h, 0).start()
            gather_copy(2 * c + h, h, 1).start()

    def gather_forward(k):
        def step(u, p):
            gather_copy(u, p, k).wait_recv()
            gather_copy(u, p, k + 2).start()
            gather_copy(u, p, k + 1).wait_recv()
            gather_copy(u, p, k + 3).start()
        return both(step)

    @both
    def gather_second(u, p):
        gather_copy(u, p, 2).wait_recv()
        gather_copy(u, p, 3).wait_recv()
        gather_copy(u, p, 4).start()
        gather_copy(u, p, 5).start()

    @both
    def gather_end(u, p):
        gather_copy(u, p, 6).wait_recv()
        gather_copy(u, p, 7).wait_recv()

    def own_hidden(c):
        gather_end(c)
        own_cot(c).wait()
        hidden(c, 0)

    def add_into(ref, other):
        ref[...] = (ref[...].astype(f32) + other[...].astype(f32)).astype(bf16)

    def work(c):
        cot_copy(c).wait_recv()

        @pl.when(c + ahead < n_chunks)
        def _():
            cot_copy(c + ahead).start()

        hidden(c, tok)
        term = lax.dot_general(
            xb[...], cb[:, chunk_cols(c)], (((0,), (0,)), ((), ())), preferred_element_type=f32
        ).astype(bf16)
        for h in range(2):
            g[2 * c + h] = term[:, h * LANES : (h + 1) * LANES].reshape(4, 4, block, LANES)
        for p in range(2):
            scatter_copy(2 * c + p, p, 0).start()
            scatter_copy(2 * c + p, p, 1).start()

    @both
    def scatter_second(u, p):
        b = second_axis[p]
        scatter_copy(u, p, 0).wait_recv()
        add_into(half2(g, u, p, after[b], 0), rah.at[u, 0])
        scatter_copy(u, p, 2).start()
        scatter_copy(u, p, 1).wait_recv()
        add_into(half2(g, u, p, before[b], 1), rah.at[u, 1])
        scatter_copy(u, p, 3).start()

    @both
    def scatter_third(u, p):
        b = second_axis[p]
        scatter_copy(u, p, 2).wait_recv()
        scatter_copy(u, p, 3).wait_recv()
        mine = seg2(g, u, p, place[b])
        mine[...] = (
            mine[...].astype(f32) + raf[u, 0].astype(f32) + raf[u, 1].astype(f32)
        ).astype(bf16)
        scatter_copy(u, p, 4).start()
        scatter_copy(u, p, 5).start()

    @both
    def scatter_fourth(u, p):
        a = first_axis[p]
        scatter_copy(u, p, 4).wait_recv()
        add_into(half1(g, u, p, after[a], 0), rbh.at[u, pl.ds(0, cut)])
        scatter_copy(u, p, 6).start()
        scatter_copy(u, p, 5).wait_recv()
        add_into(half1(g, u, p, before[a], 1), rbh.at[u, pl.ds(cut, block - cut)])
        scatter_copy(u, p, 7).start()

    @both
    def scatter_end(u, p):
        a = first_axis[p]
        scatter_copy(u, p, 6).wait_recv()
        scatter_copy(u, p, 7).wait_recv()
        mine = seg1(g, u, p, place[a])
        tmp[...] = mine[...].astype(f32) + rbf[u, 0].astype(f32) + rbf[u, 1].astype(f32)
        theirs = tmp[pl.ds(pl.multiple_of((1 - yh) * rows, 8), rows), :]
        theirs = jnp.concatenate([theirs, jnp.zeros((pad_rows - rows, LANES), f32)], axis=0)
        gps[u] = theirs.astype(bf16)
        gp_copy(u).start()
        cols = pl.ds(pl.multiple_of(my_base + u * LANES, LANES), LANES)
        g_ref[:, cols] = tmp[pl.ds(pl.multiple_of(yh * rows, 8), rows), :]

    def back_half(n, start):
        part = jnp.concatenate(
            [w[u, pl.ds(2 * n, 2)].reshape(bk_cols, LANES) for u in range(2 * n_chunks)], axis=1
        )
        return lax.dot_general(
            cb[pl.ds(start, tok), :], part, (((1,), (1,)), ((), ())), preferred_element_type=f32
        )

    def send_back(n):
        term = back_half(n, tok).astype(bf16)
        for m in range(n_bk // 2):
            i = n * (n_bk // 2) + m
            bks[i] = term[m * bk_rows : (m + 1) * bk_rows]
            bk_copy(i).start()

    def keep_back(n):
        acc[n] = back_half(n, 0)

    def tick(t):
        ranged(t, 0, gather_own)
        ranged(t, 1, gather_forward(0))
        ranged(t, 2, gather_second)
        ranged(t, 3, gather_forward(4))

        @pl.when(t == 4)
        def _():
            own_x().wait()

        ranged(t, 4, own_hidden)

        @pl.when(t == 7)
        def _():
            for c in range(ahead):
                cot_copy(c).start()

        @pl.when(t == work_lag)
        def _():
            for i in range(n_x):
                x_copy(i).wait_recv()

        ranged(t, work_lag, work)

        @pl.when((t >= done) & (t < done + 2))
        def _():
            send_back(t - done)

        @pl.when((t >= done + 2) & (t < done + 4))
        def _():
            keep_back(t - done - 2)

        ranged(t, work_lag + 3, scatter_second)
        ranged(t, work_lag + 6, scatter_third)
        ranged(t, work_lag + 8, scatter_fourth)
        ranged(t, work_lag + 9, scatter_end)

    each(n_chunks + work_lag + 9, tick)

    def finish_back(i):
        bk_copy(i).wait_recv()
        n, m = lax.div(i, n_bk // 2), lax.rem(i, n_bk // 2)
        at = pl.ds(pl.multiple_of(m * bk_rows, 16), bk_rows)
        cols = pl.ds(pl.multiple_of(n * bk_cols, LANES), bk_cols)
        out_ref[at, cols] = (acc[n, at, :] + bkr[i].astype(f32)).astype(bf16)

    each(n_bk, finish_back)

    def finish_grad(u):
        gp_copy(u).wait_recv()
        cols = pl.ds(pl.multiple_of(peer_base + u * LANES, LANES), LANES)
        g_ref[:, cols] = gpr[u].astype(f32)[:rows]

    each(2 * n_chunks, finish_grad)

    def settle(c):
        pw_copy(c).wait_send()
        cot_copy(c).wait_send()
        for p in range(2):
            u = 2 * c + p
            gp_copy(u).wait_send()
            for k in range(8):
                gather_copy(u, p, k).wait_send()
                scatter_copy(u, p, k).wait_send()

    each(n_chunks, settle)
    each(n_x, lambda i: x_copy(i).wait_send())
    each(n_bk, lambda i: bk_copy(i).wait_send())


def projection(acts, cot, weights):
    tok, width = acts.shape
    rows, ffw = weights.shape
    units = ffw // 2 // LANES
    chunks = units // 2
    block = 2 * rows
    pad_rows = (rows + 15) // 16 * 16
    n_x, n_bk = 3, 6
    dma = pltpu.SemaphoreType.DMA
    vmem = pltpu.VMEM
    return pl.pallas_call(
        pair_kernel,
        out_shape=(
            jax.ShapeDtypeStruct((tok, width), bf16),
            jax.ShapeDtypeStruct((rows, ffw), f32),
        ),
        in_specs=[
            pl.BlockSpec(memory_space=pl.ANY),
            pl.BlockSpec(memory_space=pl.ANY),
            pl.BlockSpec(memory_space=pltpu.VMEM),
        ],
        out_specs=(
            pl.BlockSpec(memory_space=pltpu.VMEM),
            pl.BlockSpec(memory_space=pltpu.VMEM),
        ),
        scratch_shapes=[
            vmem((2 * tok, width), bf16),
            vmem((2 * tok, ffw // 2), bf16),
            vmem((units, 4, 4, block, LANES), bf16),
            vmem((units, 4, 4, block, LANES), bf16),
            vmem((units, 2, 2, block, LANES), bf16),
            vmem((units, 2, 4, block, LANES), bf16),
            vmem((units, block, LANES), bf16),
            vmem((units, 2, block, LANES), bf16),
            vmem((chunks, 2, pad_rows, LANES), bf16),
            vmem((chunks, 2, pad_rows, LANES), bf16),
            vmem((units, pad_rows, LANES), bf16),
            vmem((units, pad_rows, LANES), bf16),
            vmem((n_bk, tok // (n_bk // 2), width // 2), bf16),
            vmem((n_bk, tok // (n_bk // 2), width // 2), bf16),
            vmem((block, LANES), f32),
            vmem((2, tok, width // 2), f32),
            dma((chunks + 1,)),
            dma((units, 8)), dma((units, 8)),
            dma((units, 8)), dma((units, 8)),
            dma((chunks,)), dma((chunks,)),
            dma((n_x,)), dma((n_x,)),
            dma((chunks,)), dma((chunks,)),
            dma((n_bk,)), dma((n_bk,)),
            dma((units,)), dma((units,)),
        ],
        compiler_params=pltpu.CompilerParams(
            collective_id=1, has_side_effects=True, vmem_limit_bytes=60 * 2**20
        ),
        cost_estimate=pl.CostEstimate(
            flops=6 * tok * width * ffw, bytes_accessed=16 * tok * width, transcendentals=tok * ffw
        ),
        name="pair_projection",
    )(acts, cot, weights)


def body(inputs, cotangent, params, first_moment, second_moment, snapshot, momentum, fragment):
    weights = params[0]
    frag = snapshot.shape[1]
    start_col = fragment[0] * frag
    local = lax.dynamic_slice_in_dim(weights, start_col, frag, 1)
    total = lax.psum((snapshot - local).astype(bf16), "rep").astype(f32)
    input_grad, grad = projection(inputs[0], cotangent[0], weights)
    outer_grad = total / lax.axis_size("rep")
    new_momentum = outer_mu * momentum + outer_grad
    new_snapshot = snapshot - outer_rate * (outer_grad + outer_mu * new_momentum)
    first = beta_one * first_moment[0] + (1.0 - beta_one) * grad
    second = beta_two * second_moment[0] + (1.0 - beta_two) * grad * grad
    stepped = weights - inner_rate * (first / (jnp.sqrt(second) + adam_eps) + decay_rate * weights)
    frag_part = lax.dynamic_slice_in_dim(stepped, start_col, frag, 1)
    merged = mix_rate * new_snapshot + (1.0 - mix_rate) * frag_part
    stepped = lax.dynamic_update_slice_in_dim(stepped, merged, start_col, 1)
    return (stepped[None], first[None], second[None], input_grad[None], new_momentum, new_snapshot)


def solution(mesh):
    return jax.shard_map(
        body,
        mesh=mesh,
        in_specs=(
            P("rep", "fsdp", None),
            P("rep", "fsdp", None),
            P("rep", "fsdp", None),
            P("rep", "fsdp", None),
            P("rep", "fsdp", None),
            P("fsdp", None),
            P("fsdp", None),
            P(),
        ),
        out_specs=(
            P("rep", "fsdp", None),
            P("rep", "fsdp", None),
            P("rep", "fsdp", None),
            P("rep", "fsdp", None),
            P("fsdp", None),
            P("fsdp", None),
        ),
        check_vma=False,
    )
```

```python
import functools

import jax
import jax.numpy as jnp
from jax import lax
from jax.experimental import pallas as pl
from jax.experimental.pallas import tpu as pltpu
from jax.sharding import PartitionSpec as P

beta_one = 0.9
beta_two = 0.95
inner_rate = 0.01
adam_eps = 1e-08
decay_rate = 0.1
outer_rate = 0.7
outer_mu = 0.9
mix_rate = 0.5

LANES = 128
CHUNK = 256
MESH = pl.DeviceIdType.MESH
f32 = jnp.float32
bf16 = jnp.bfloat16


def gelu_slope(t):
    c = 0.7978845608028654
    sq = t * t
    th = jnp.tanh(c * t * (1.0 + 0.044715 * sq))
    return 0.5 * (1.0 + th) + 0.5 * t * (1.0 - th * th) * (c * (1.0 + 3 * 0.044715 * sq))


def pair_kernel(
    frag_ref, x_hbm, cot_hbm, p_ref, snap_ref,
    out_ref, g_ref, total_ref,
    xb, cb, w, g, rah, raf, rbh, rbf, pws, pwr, gps, gpr, bks, bkr, tmp, acc, pair_tmp, ds, dr,
    loc_sem, ag_send, ag_recv, rs_send, rs_recv, pw_send, pw_recv,
    x_send, x_recv, cot_send, cot_recv, bk_send, bk_recv, gp_send, gp_recv, d_send, d_recv,
):
    tok, width = x_hbm.shape
    rows, ffw = p_ref.shape
    half_cols = ffw // 2
    n_chunks = half_cols // CHUNK
    block = 2 * rows
    pad_rows = ds.shape[1]
    frag = snap_ref.shape[1]
    cut = (block // 16 + 1) // 2 * 16
    n_x = x_send.shape[0]
    x_rows = tok // n_x
    n_bk = bk_send.shape[0]
    bk_rows = tok // (n_bk // 2)
    bk_cols = width // 2
    scale = width ** (-0.5)
    ahead = 6
    work_lag = 10
    done = work_lag + n_chunks

    f = lax.axis_index("fsdp")
    r = lax.axis_index("rep")
    yh = lax.rem(f, 2)
    x = lax.rem(lax.div(f, 2), 4)
    z = lax.div(f, 8)

    def device(zz, xx, yy):
        return {"fsdp": zz * 8 + xx * 2 + yy}

    peer = device(z, x, 1 - yh)
    sibling = {"rep": r + 1 - 2 * lax.rem(r, 2)}
    neighbour = {"rep": lax.rem(r + 2, 4)}
    place = {"x": x, "z": z}
    after = {a: lax.rem(place[a] + 1, 4) for a in place}
    before = {a: lax.rem(place[a] + 3, 4) for a in place}
    across = {a: lax.rem(place[a] + 2, 4) for a in place}
    right = {"x": device(z, after["x"], yh), "z": device(after["z"], x, yh)}
    left = {"x": device(z, before["x"], yh), "z": device(before["z"], x, yh)}
    first_axis = ("x", "z")
    second_axis = ("z", "x")
    my_base = yh * half_cols
    peer_base = (1 - yh) * half_cols

    def seg2(ref, u, p, i):
        return ref.at[u, i] if p == 0 else ref.at[u, :, i]

    def half2(ref, u, p, i, h):
        part = pl.ds(2 * h, 2)
        return ref.at[u, i, part] if p == 0 else ref.at[u, part, i]

    def seg1(ref, u, p, i):
        return ref.at[u, z, i] if p == 0 else ref.at[u, i, x]

    def half1(ref, u, p, i, h):
        part = pl.ds(0, cut) if h == 0 else pl.ds(cut, block - cut)
        return ref.at[u, z, i, part] if p == 0 else ref.at[u, i, x, part]

    def chunk_cols(c):
        return pl.ds(pl.multiple_of(c * CHUNK, CHUNK), CHUNK)

    def remote(src, dst, send, recv, to):
        return pltpu.make_async_remote_copy(
            src_ref=src, dst_ref=dst, send_sem=send, recv_sem=recv, device_id=to, device_id_type=MESH
        )

    def gather_copy(u, p, k):
        a, b = first_axis[p], second_axis[p]
        part = (
            lambda: seg1(w, u, p, place[a]),
            lambda: seg1(w, u, p, place[a]),
            lambda: half1(w, u, p, before[a], 0),
            lambda: half1(w, u, p, after[a], 1),
            lambda: seg2(w, u, p, place[b]),
            lambda: seg2(w, u, p, place[b]),
            lambda: half2(w, u, p, before[b], 0),
            lambda: half2(w, u, p, after[b], 1),
        )[k]()
        to = (right if k % 2 == 0 else left)[a if k < 4 else b]
        return remote(part, part, ag_send.at[u, k], ag_recv.at[u, k], to)

    def scatter_copy(u, p, k):
        a, b = first_axis[p], second_axis[p]
        src, dst = (
            lambda: (half2(g, u, p, across[b], 0), rah.at[u, 0]),
            lambda: (half2(g, u, p, across[b], 1), rah.at[u, 1]),
            lambda: (seg2(g, u, p, after[b]), raf.at[u, 0]),
            lambda: (seg2(g, u, p, before[b]), raf.at[u, 1]),
            lambda: (half1(g, u, p, across[a], 0), rbh.at[u, pl.ds(0, cut)]),
            lambda: (half1(g, u, p, across[a], 1), rbh.at[u, pl.ds(cut, block - cut)]),
            lambda: (seg1(g, u, p, after[a]), rbf.at[u, 0]),
            lambda: (seg1(g, u, p, before[a]), rbf.at[u, 1]),
        )[k]()
        to = (right if k % 2 == 0 else left)[b if k < 4 else a]
        return remote(src, dst, rs_send.at[u, k], rs_recv.at[u, k], to)

    def pw_copy(c):
        return remote(pws.at[c], pwr.at[c], pw_send.at[c], pw_recv.at[c], peer)

    def x_copy(i):
        return remote(
            x_hbm.at[pl.ds(i * x_rows, x_rows)], xb.at[pl.ds(tok + i * x_rows, x_rows)],
            x_send.at[i], x_recv.at[i], peer,
        )

    def cot_copy(c):
        cols = pl.ds(pl.multiple_of(peer_base + c * CHUNK, CHUNK), CHUNK)
        return remote(
            cot_hbm.at[:, cols], cb.at[pl.ds(tok, tok), chunk_cols(c)],
            cot_send.at[c], cot_recv.at[c], peer,
        )

    def bk_copy(i):
        return remote(bks.at[i], bkr.at[i], bk_send.at[i], bk_recv.at[i], peer)

    def gp_copy(c):
        return remote(gps.at[c], gpr.at[c], gp_send.at[c], gp_recv.at[c], peer)

    def d_copy(i):
        return remote(ds.at[i], dr.at[i], d_send.at[i], d_recv.at[i], (sibling, neighbour)[i])

    def own_x():
        return pltpu.make_async_copy(x_hbm, xb.at[pl.ds(0, tok)], loc_sem.at[n_chunks])

    def own_cot(c):
        cols = pl.ds(pl.multiple_of(my_base + c * CHUNK, CHUNK), CHUNK)
        return pltpu.make_async_copy(
            cot_hbm.at[:, cols], cb.at[pl.ds(0, tok), chunk_cols(c)], loc_sem.at[c]
        )

    def each(count, step):
        def run(i, carry):
            step(i)
            return carry
        lax.fori_loop(0, count, run, 0)

    def ranged(t, lag, step):
        @pl.when((t >= lag) & (t < lag + n_chunks))
        def _():
            step(t - lag)

    def both(step):
        def run(c):
            for p in range(2):
                step(2 * c + p, p)
        return run

    own_x().start()
    each(n_chunks, lambda c: own_cot(c).start())

    def prepare(c):
        parts = []
        for h in range(2):
            cols = pl.ds(pl.multiple_of(peer_base + c * CHUNK + h * LANES, LANES), LANES)
            parts.append(p_ref[:, cols])
        pws[c] = jnp.concatenate(parts, axis=0).astype(bf16)

    each(n_chunks, prepare)
    local = p_ref[:, :frag]
    for i in range(1, ffw // frag):
        local = jnp.where(frag_ref[0] == i, p_ref[:, i * frag : (i + 1) * frag], local)
    delta = snap_ref[...] - local
    ds[0] = jnp.concatenate([delta, jnp.zeros((pad_rows - rows, frag), f32)], axis=0).astype(bf16)

    barrier = pltpu.get_barrier_semaphore()
    partners = (peer, right["x"], left["x"], right["z"], left["z"], sibling, neighbour)
    for partner in partners:
        pl.semaphore_signal(barrier, inc=1, device_id=partner, device_id_type=MESH)
    pl.semaphore_wait(barrier, len(partners))

    each(n_chunks, lambda c: pw_copy(c).start())
    each(n_x, lambda i: x_copy(i).start())
    d_copy(0).start()

    def chunk_weights(c):
        return jnp.concatenate(
            [w[2 * c].reshape(width, LANES), w[2 * c + 1].reshape(width, LANES)], axis=1
        )

    def hidden(c, start):
        at = pl.ds(start, tok)
        pre = jnp.dot(xb[at, :], chunk_weights(c), preferred_element_type=f32) * scale
        cot = cb[at, chunk_cols(c)].astype(f32)
        cb[at, chunk_cols(c)] = (gelu_slope(pre) * cot * scale).astype(bf16)

    def gather_own(c):
        pw_copy(c).wait_recv()
        pair_tmp[...] = pwr[c].astype(f32)
        for h in range(2):
            cols = pl.ds(pl.multiple_of(my_base + c * CHUNK + h * LANES, LANES), LANES)
            tmp[pl.ds(pl.multiple_of(yh * rows, 8), rows), :] = p_ref[:, cols]
            tmp[pl.ds(pl.multiple_of((1 - yh) * rows, 8), rows), :] = pair_tmp[pl.ds(h * rows, rows), :]
            w[2 * c + h, z, x] = tmp[...].astype(bf16)
            gather_copy(2 * c + h, h, 0).start()
            gather_copy(2 * c + h, h, 1).start()

    def gather_forward(k):
        def step(u, p):
            gather_copy(u, p, k).wait_recv()
            gather_copy(u, p, k + 2).start()
            gather_copy(u, p, k + 1).wait_recv()
            gather_copy(u, p, k + 3).start()
        return both(step)

    @both
    def gather_second(u, p):
        gather_copy(u, p, 2).wait_recv()
        gather_copy(u, p, 3).wait_recv()
        gather_copy(u, p, 4).start()
        gather_copy(u, p, 5).start()

    @both
    def gather_end(u, p):
        gather_copy(u, p, 6).wait_recv()
        gather_copy(u, p, 7).wait_recv()

    def own_hidden(c):
        gather_end(c)
        own_cot(c).wait()
        hidden(c, 0)

    def add_into(ref, other):
        ref[...] = (ref[...].astype(f32) + other[...].astype(f32)).astype(bf16)

    def back_half(n, start):
        part = jnp.concatenate(
            [w[u, pl.ds(2 * n, 2)].reshape(bk_cols, LANES) for u in range(2 * n_chunks)], axis=1
        )
        return lax.dot_general(
            cb[pl.ds(start, tok), :], part, (((1,), (1,)), ((), ())), preferred_element_type=f32
        )

    def send_back(n):
        term = back_half(n, tok).astype(bf16)
        for m in range(n_bk // 2):
            i = n * (n_bk // 2) + m
            bks[i] = term[m * bk_rows : (m + 1) * bk_rows]
            bk_copy(i).start()

    def work(c):
        cot_copy(c).wait_recv()

        @pl.when(c + ahead < n_chunks)
        def _():
            cot_copy(c + ahead).start()

        hidden(c, tok)

        @pl.when(c == n_chunks - 1)
        def _():
            send_back(0)

        term = lax.dot_general(
            xb[...], cb[:, chunk_cols(c)], (((0,), (0,)), ((), ())), preferred_element_type=f32
        ).astype(bf16)
        for h in range(2):
            g[2 * c + h] = term[:, h * LANES : (h + 1) * LANES].reshape(4, 4, block, LANES)
        for p in range(2):
            scatter_copy(2 * c + p, p, 0).start()
            scatter_copy(2 * c + p, p, 1).start()

    @both
    def scatter_second(u, p):
        b = second_axis[p]
        scatter_copy(u, p, 0).wait_recv()
        add_into(half2(g, u, p, after[b], 0), rah.at[u, 0])
        scatter_copy(u, p, 2).start()
        scatter_copy(u, p, 1).wait_recv()
        add_into(half2(g, u, p, before[b], 1), rah.at[u, 1])
        scatter_copy(u, p, 3).start()

    @both
    def scatter_third(u, p):
        b = second_axis[p]
        scatter_copy(u, p, 2).wait_recv()
        scatter_copy(u, p, 3).wait_recv()
        mine = seg2(g, u, p, place[b])
        mine[...] = (
            mine[...].astype(f32) + raf[u, 0].astype(f32) + raf[u, 1].astype(f32)
        ).astype(bf16)
        scatter_copy(u, p, 4).start()
        scatter_copy(u, p, 5).start()

    @both
    def scatter_fourth(u, p):
        a = first_axis[p]
        scatter_copy(u, p, 4).wait_recv()
        add_into(half1(g, u, p, after[a], 0), rbh.at[u, pl.ds(0, cut)])
        scatter_copy(u, p, 6).start()
        scatter_copy(u, p, 5).wait_recv()
        add_into(half1(g, u, p, before[a], 1), rbh.at[u, pl.ds(cut, block - cut)])
        scatter_copy(u, p, 7).start()

    @both
    def scatter_end(u, p):
        a = first_axis[p]
        scatter_copy(u, p, 6).wait_recv()
        scatter_copy(u, p, 7).wait_recv()
        mine = seg1(g, u, p, place[a])
        tmp[...] = mine[...].astype(f32) + rbf[u, 0].astype(f32) + rbf[u, 1].astype(f32)
        pair_tmp[pl.ds(p * rows, rows), :] = tmp[pl.ds(pl.multiple_of((1 - yh) * rows, 8), rows), :]
        cols = pl.ds(pl.multiple_of(my_base + u * LANES, LANES), LANES)
        g_ref[:, cols] = tmp[pl.ds(pl.multiple_of(yh * rows, 8), rows), :]
        if p == 1:
            c = lax.div(u, 2)
            gps[c] = pair_tmp[...].astype(bf16)
            gp_copy(c).start()

    def keep_back(n):
        acc[n] = back_half(n, 0)

    def tick(t):
        ranged(t, 0, gather_own)
        ranged(t, 1, gather_forward(0))
        ranged(t, 2, gather_second)
        ranged(t, 3, gather_forward(4))

        @pl.when(t == 4)
        def _():
            own_x().wait()

        ranged(t, 4, own_hidden)

        @pl.when(t == 1)
        def _():
            d_copy(0).wait_recv()
            ds[1] = (ds[0].astype(f32) + dr[0].astype(f32)).astype(bf16)

        @pl.when(t == work_lag + 2)
        def _():
            d_copy(1).start()

        @pl.when(t == 8)
        def _():
            for c in range(ahead):
                cot_copy(c).start()

        @pl.when(t == work_lag)
        def _():
            for i in range(n_x):
                x_copy(i).wait_recv()

        ranged(t, work_lag, work)

        @pl.when(t == done)
        def _():
            send_back(1)

        @pl.when((t >= done + 1) & (t < done + 3))
        def _():
            keep_back(t - done - 1)

        ranged(t, work_lag + 3, scatter_second)
        ranged(t, work_lag + 6, scatter_third)
        ranged(t, work_lag + 8, scatter_fourth)
        ranged(t, work_lag + 9, scatter_end)

    each(n_chunks + work_lag + 9, tick)

    def finish_back(i):
        bk_copy(i).wait_recv()
        n, m = lax.div(i, n_bk // 2), lax.rem(i, n_bk // 2)
        at = pl.ds(pl.multiple_of(m * bk_rows, 16), bk_rows)
        cols = pl.ds(pl.multiple_of(n * bk_cols, LANES), bk_cols)
        out_ref[at, cols] = (acc[n, at, :] + bkr[i].astype(f32)).astype(bf16)

    each(n_bk, finish_back)

    def finish_grad(c):
        gp_copy(c).wait_recv()
        pair_tmp[...] = gpr[c].astype(f32)
        for h in range(2):
            cols = pl.ds(pl.multiple_of(peer_base + c * CHUNK + h * LANES, LANES), LANES)
            g_ref[:, cols] = pair_tmp[pl.ds(h * rows, rows), :]

    d_copy(1).wait_recv()
    total_ref[...] = (ds[1].astype(f32) + dr[1].astype(f32))[:rows]
    each(n_chunks, finish_grad)

    def settle(c):
        pw_copy(c).wait_send()
        cot_copy(c).wait_send()
        gp_copy(c).wait_send()
        for p in range(2):
            u = 2 * c + p
            for k in range(8):
                gather_copy(u, p, k).wait_send()
                scatter_copy(u, p, k).wait_send()

    each(n_chunks, settle)
    each(n_x, lambda i: x_copy(i).wait_send())
    each(n_bk, lambda i: bk_copy(i).wait_send())
    for i in range(2):
        d_copy(i).wait_send()


def projection(fragment, acts, cot, weights, snapshot):
    tok, width = acts.shape
    rows, ffw = weights.shape
    frag = snapshot.shape[1]
    units = ffw // 2 // LANES
    chunks = units // 2
    block = 2 * rows
    pad_rows = (rows + 15) // 16 * 16
    n_x, n_bk = 3, 6
    dma = pltpu.SemaphoreType.DMA
    vmem = pltpu.VMEM
    return pl.pallas_call(
        pair_kernel,
        out_shape=(
            jax.ShapeDtypeStruct((tok, width), bf16),
            jax.ShapeDtypeStruct((rows, ffw), f32),
            jax.ShapeDtypeStruct((rows, frag), f32),
        ),
        in_specs=[
            pl.BlockSpec(memory_space=pltpu.SMEM),
            pl.BlockSpec(memory_space=pl.ANY),
            pl.BlockSpec(memory_space=pl.ANY),
            pl.BlockSpec(memory_space=pltpu.VMEM),
            pl.BlockSpec(memory_space=pltpu.VMEM),
        ],
        out_specs=(
            pl.BlockSpec(memory_space=pltpu.VMEM),
            pl.BlockSpec(memory_space=pltpu.VMEM),
            pl.BlockSpec(memory_space=pltpu.VMEM),
        ),
        scratch_shapes=[
            vmem((2 * tok, width), bf16),
            vmem((2 * tok, ffw // 2), bf16),
            vmem((units, 4, 4, block, LANES), bf16),
            vmem((units, 4, 4, block, LANES), bf16),
            vmem((units, 2, 2, block, LANES), bf16),
            vmem((units, 2, 4, block, LANES), bf16),
            vmem((units, block, LANES), bf16),
            vmem((units, 2, block, LANES), bf16),
            vmem((chunks, block, LANES), bf16),
            vmem((chunks, block, LANES), bf16),
            vmem((chunks, block, LANES), bf16),
            vmem((chunks, block, LANES), bf16),
            vmem((n_bk, tok // (n_bk // 2), width // 2), bf16),
            vmem((n_bk, tok // (n_bk // 2), width // 2), bf16),
            vmem((block, LANES), f32),
            vmem((2, tok, width // 2), f32),
            vmem((block, LANES), f32),
            vmem((2, pad_rows, frag), bf16),
            vmem((2, pad_rows, frag), bf16),
            dma((chunks + 1,)),
            dma((units, 8)), dma((units, 8)),
            dma((units, 8)), dma((units, 8)),
            dma((chunks,)), dma((chunks,)),
            dma((n_x,)), dma((n_x,)),
            dma((chunks,)), dma((chunks,)),
            dma((n_bk,)), dma((n_bk,)),
            dma((chunks,)), dma((chunks,)),
            dma((2,)), dma((2,)),
        ],
        compiler_params=pltpu.CompilerParams(
            collective_id=1, has_side_effects=True, vmem_limit_bytes=60 * 2**20
        ),
        cost_estimate=pl.CostEstimate(
            flops=6 * tok * width * ffw, bytes_accessed=16 * tok * width, transcendentals=tok * ffw
        ),
        name="pair_projection",
    )(fragment, acts, cot, weights, snapshot)


def update_kernel(
    frag_ref, g_ref, p_ref, m_ref, v_ref, snap_ref, mom_ref, total_ref,
    new_p, new_m, new_v, new_mom, new_snap,
):
    step = pl.program_id(0)

    @pl.when(step == 0)
    def _():
        outer = total_ref[...] * 0.25
        mom = outer_mu * mom_ref[...] + outer
        new_mom[...] = mom
        new_snap[...] = snap_ref[...] - outer_rate * (outer + outer_mu * mom)

    grad = g_ref[...]
    weights = p_ref[...]
    first = beta_one * m_ref[...] + (1.0 - beta_one) * grad
    second = beta_two * v_ref[...] + (1.0 - beta_two) * grad * grad
    new_m[...] = first
    new_v[...] = second
    stepped = weights - inner_rate * (first / (jnp.sqrt(second) + adam_eps) + decay_rate * weights)
    new_p[...] = stepped

    @pl.when(step == frag_ref[0])
    def _():
        new_p[...] = mix_rate * new_snap[...] + (1.0 - mix_rate) * new_p[...]


def update(fragment, grad, weights, first, second, snapshot, momentum, total):
    rows, ffw = weights.shape
    frag = snapshot.shape[1]
    wide = pl.BlockSpec((rows, frag), lambda j: (0, j))
    fixed = pl.BlockSpec((rows, frag), lambda j: (0, 0))
    full = jax.ShapeDtypeStruct((rows, ffw), f32)
    part = jax.ShapeDtypeStruct((rows, frag), f32)
    return pl.pallas_call(
        update_kernel,
        grid=(ffw // frag,),
        in_specs=[pl.BlockSpec(memory_space=pltpu.SMEM)] + [wide] * 4 + [fixed] * 3,
        out_specs=[wide] * 3 + [fixed] * 2,
        out_shape=[full] * 3 + [part] * 2,
        compiler_params=pltpu.CompilerParams(vmem_limit_bytes=60 * 2**20),
        name="update",
    )(fragment, grad, weights, first, second, snapshot, momentum, total)


def body(inputs, cotangent, params, first_moment, second_moment, snapshot, momentum, fragment):
    input_grad, grad, total = projection(fragment, inputs[0], cotangent[0], params[0], snapshot)
    stepped, first, second, new_momentum, new_snapshot = update(
        fragment, grad, params[0], first_moment[0], second_moment[0], snapshot, momentum, total
    )
    return (stepped[None], first[None], second[None], input_grad[None], new_momentum, new_snapshot)


def solution(mesh):
    return jax.shard_map(
        body,
        mesh=mesh,
        in_specs=(
            P("rep", "fsdp", None),
            P("rep", "fsdp", None),
            P("rep", "fsdp", None),
            P("rep", "fsdp", None),
            P("rep", "fsdp", None),
            P("fsdp", None),
            P("fsdp", None),
            P(),
        ),
        out_specs=(
            P("rep", "fsdp", None),
            P("rep", "fsdp", None),
            P("rep", "fsdp", None),
            P("rep", "fsdp", None),
            P("fsdp", None),
            P("fsdp", None),
        ),
        check_vma=False,
    )
```

```python
import functools

import jax
import jax.numpy as jnp
from jax import lax
from jax.experimental import pallas as pl
from jax.experimental.pallas import tpu as pltpu
from jax.sharding import PartitionSpec as P

beta_one = 0.9
beta_two = 0.95
inner_rate = 0.01
adam_eps = 1e-08
decay_rate = 0.1
outer_rate = 0.7
outer_mu = 0.9
mix_rate = 0.5

LANES = 128
CHUNK = 256
MESH = pl.DeviceIdType.MESH
f32 = jnp.float32
bf16 = jnp.bfloat16


def gelu_slope(t):
    c = 0.7978845608028654
    sq = t * t
    th = jnp.tanh(c * t * (1.0 + 0.044715 * sq))
    return 0.5 * (1.0 + th) + 0.5 * t * (1.0 - th * th) * (c * (1.0 + 3 * 0.044715 * sq))


def pair_kernel(
    frag_ref, x_hbm, cot_hbm, p_hbm, snap_hbm,
    out_hbm, g_hbm, total_hbm,
    p_ref, snap_ref, out_ref, g_ref, total_ref,
    xb, cb, w, g, rah, raf, rbh, rbf, pws, pwr, gps, gpr, bks, bkr, tmp, acc, pair_tmp, ds, dr,
    loc_sem, ag_send, ag_recv, rs_send, rs_recv, pw_send, pw_recv,
    x_send, x_recv, cot_send, cot_recv, bk_send, bk_recv, gp_send, gp_recv, d_send, d_recv,
    out_sem, g_sem, total_sem,
):
    tok, width = x_hbm.shape
    rows, ffw = p_ref.shape
    half_cols = ffw // 2
    n_chunks = half_cols // CHUNK
    block = 2 * rows
    pad_rows = ds.shape[1]
    frag = snap_ref.shape[1]
    cut = (block // 16 + 1) // 2 * 16
    n_x = x_send.shape[0]
    x_rows = tok // n_x
    n_bk = bk_send.shape[0]
    bk_rows = tok // (n_bk // 2)
    bk_cols = width // 2
    scale = width ** (-0.5)
    ahead = 6
    work_lag = 10
    done = work_lag + n_chunks

    f = lax.axis_index("fsdp")
    r = lax.axis_index("rep")
    yh = lax.rem(f, 2)
    x = lax.rem(lax.div(f, 2), 4)
    z = lax.div(f, 8)

    def device(zz, xx, yy):
        return {"fsdp": zz * 8 + xx * 2 + yy}

    peer = device(z, x, 1 - yh)
    sibling = {"rep": r + 1 - 2 * lax.rem(r, 2)}
    neighbour = {"rep": lax.rem(r + 2, 4)}
    place = {"x": x, "z": z}
    after = {a: lax.rem(place[a] + 1, 4) for a in place}
    before = {a: lax.rem(place[a] + 3, 4) for a in place}
    across = {a: lax.rem(place[a] + 2, 4) for a in place}
    right = {"x": device(z, after["x"], yh), "z": device(after["z"], x, yh)}
    left = {"x": device(z, before["x"], yh), "z": device(before["z"], x, yh)}
    first_axis = ("x", "z")
    second_axis = ("z", "x")
    my_base = yh * half_cols
    peer_base = (1 - yh) * half_cols

    def seg2(ref, u, p, i):
        return ref.at[u, i] if p == 0 else ref.at[u, :, i]

    def half2(ref, u, p, i, h):
        part = pl.ds(2 * h, 2)
        return ref.at[u, i, part] if p == 0 else ref.at[u, part, i]

    def seg1(ref, u, p, i):
        return ref.at[u, z, i] if p == 0 else ref.at[u, i, x]

    def half1(ref, u, p, i, h):
        part = pl.ds(0, cut) if h == 0 else pl.ds(cut, block - cut)
        return ref.at[u, z, i, part] if p == 0 else ref.at[u, i, x, part]

    def chunk_cols(c):
        return pl.ds(pl.multiple_of(c * CHUNK, CHUNK), CHUNK)

    def remote(src, dst, send, recv, to):
        return pltpu.make_async_remote_copy(
            src_ref=src, dst_ref=dst, send_sem=send, recv_sem=recv, device_id=to, device_id_type=MESH
        )

    def gather_copy(u, p, k):
        a, b = first_axis[p], second_axis[p]
        part = (
            lambda: seg1(w, u, p, place[a]),
            lambda: seg1(w, u, p, place[a]),
            lambda: half1(w, u, p, before[a], 0),
            lambda: half1(w, u, p, after[a], 1),
            lambda: seg2(w, u, p, place[b]),
            lambda: seg2(w, u, p, place[b]),
            lambda: half2(w, u, p, before[b], 0),
            lambda: half2(w, u, p, after[b], 1),
        )[k]()
        to = (right if k % 2 == 0 else left)[a if k < 4 else b]
        return remote(part, part, ag_send.at[u, k], ag_recv.at[u, k], to)

    def scatter_copy(u, p, k):
        a, b = first_axis[p], second_axis[p]
        src, dst = (
            lambda: (half2(g, u, p, across[b], 0), rah.at[u, 0]),
            lambda: (half2(g, u, p, across[b], 1), rah.at[u, 1]),
            lambda: (seg2(g, u, p, after[b]), raf.at[u, 0]),
            lambda: (seg2(g, u, p, before[b]), raf.at[u, 1]),
            lambda: (half1(g, u, p, across[a], 0), rbh.at[u, pl.ds(0, cut)]),
            lambda: (half1(g, u, p, across[a], 1), rbh.at[u, pl.ds(cut, block - cut)]),
            lambda: (seg1(g, u, p, after[a]), rbf.at[u, 0]),
            lambda: (seg1(g, u, p, before[a]), rbf.at[u, 1]),
        )[k]()
        to = (right if k % 2 == 0 else left)[b if k < 4 else a]
        return remote(src, dst, rs_send.at[u, k], rs_recv.at[u, k], to)

    def pw_copy(c):
        return remote(pws.at[c], pwr.at[c], pw_send.at[c], pw_recv.at[c], peer)

    def x_copy(i):
        return remote(
            x_hbm.at[pl.ds(i * x_rows, x_rows)], xb.at[pl.ds(tok + i * x_rows, x_rows)],
            x_send.at[i], x_recv.at[i], peer,
        )

    def cot_copy(c):
        cols = pl.ds(pl.multiple_of(peer_base + c * CHUNK, CHUNK), CHUNK)
        return remote(
            cot_hbm.at[:, cols], cb.at[pl.ds(tok, tok), chunk_cols(c)],
            cot_send.at[c], cot_recv.at[c], peer,
        )

    def bk_copy(i):
        return remote(bks.at[i], bkr.at[i], bk_send.at[i], bk_recv.at[i], peer)

    def gp_copy(c):
        return remote(gps.at[c], gpr.at[c], gp_send.at[c], gp_recv.at[c], peer)

    def g_out(c, base, h):
        cols = pl.ds(pl.multiple_of(base + c * CHUNK, CHUNK), CHUNK)
        return pltpu.make_async_copy(g_ref.at[:, cols], g_hbm.at[:, cols], g_sem.at[2 * c + h])

    def total_out():
        return pltpu.make_async_copy(total_ref, total_hbm, total_sem.at[0])

    def back_out(i):
        n, m = lax.div(i, n_bk // 2), lax.rem(i, n_bk // 2)
        at = pl.ds(pl.multiple_of(m * bk_rows, 16), bk_rows)
        cols = pl.ds(pl.multiple_of(n * bk_cols, LANES), bk_cols)
        return pltpu.make_async_copy(out_ref.at[at, cols], out_hbm.at[at, cols], out_sem.at[i])

    def d_copy(i):
        return remote(ds.at[i], dr.at[i], d_send.at[i], d_recv.at[i], (sibling, neighbour)[i])

    def own_x():
        return pltpu.make_async_copy(x_hbm, xb.at[pl.ds(0, tok)], loc_sem.at[n_chunks])

    def own_params():
        return pltpu.make_async_copy(p_hbm, p_ref, loc_sem.at[n_chunks + 1])

    def own_snap():
        return pltpu.make_async_copy(snap_hbm, snap_ref, loc_sem.at[n_chunks + 2])

    def own_cot(c):
        cols = pl.ds(pl.multiple_of(my_base + c * CHUNK, CHUNK), CHUNK)
        return pltpu.make_async_copy(
            cot_hbm.at[:, cols], cb.at[pl.ds(0, tok), chunk_cols(c)], loc_sem.at[c]
        )

    def each(count, step):
        def run(i, carry):
            step(i)
            return carry
        lax.fori_loop(0, count, run, 0)

    def ranged(t, lag, step):
        @pl.when((t >= lag) & (t < lag + n_chunks))
        def _():
            step(t - lag)

    def both(step):
        def run(c):
            for p in range(2):
                step(2 * c + p, p)
        return run

    barrier = pltpu.get_barrier_semaphore()
    partners = (peer, right["x"], left["x"], right["z"], left["z"], sibling, neighbour)
    for partner in partners:
        pl.semaphore_signal(barrier, inc=1, device_id=partner, device_id_type=MESH)
    own_params().start()
    own_snap().start()
    own_x().start()
    each(n_chunks, lambda c: own_cot(c).start())
    own_params().wait()
    pl.semaphore_wait(barrier, len(partners))

    def prepare(c):
        parts = []
        for h in range(2):
            cols = pl.ds(pl.multiple_of(peer_base + c * CHUNK + h * LANES, LANES), LANES)
            parts.append(p_ref[:, cols])
        pws[c] = jnp.concatenate(parts, axis=0).astype(bf16)
        pw_copy(c).start()

    each(n_chunks, prepare)
    each(n_x, lambda i: x_copy(i).start())
    own_snap().wait()
    local = p_ref[:, :frag]
    for i in range(1, ffw // frag):
        local = jnp.where(frag_ref[0] == i, p_ref[:, i * frag : (i + 1) * frag], local)
    delta = snap_ref[...] - local
    ds[0] = jnp.concatenate([delta, jnp.zeros((pad_rows - rows, frag), f32)], axis=0).astype(bf16)

    d_copy(0).start()

    def chunk_weights(c):
        return jnp.concatenate(
            [w[2 * c].reshape(width, LANES), w[2 * c + 1].reshape(width, LANES)], axis=1
        )

    def hidden(c, start):
        at = pl.ds(start, tok)
        pre = jnp.dot(xb[at, :], chunk_weights(c), preferred_element_type=f32) * scale
        cot = cb[at, chunk_cols(c)].astype(f32)
        cb[at, chunk_cols(c)] = (gelu_slope(pre) * cot * scale).astype(bf16)

    def gather_own(c):
        pw_copy(c).wait_recv()
        pair_tmp[...] = pwr[c].astype(f32)
        for h in range(2):
            cols = pl.ds(pl.multiple_of(my_base + c * CHUNK + h * LANES, LANES), LANES)
            tmp[pl.ds(pl.multiple_of(yh * rows, 8), rows), :] = p_ref[:, cols]
            tmp[pl.ds(pl.multiple_of((1 - yh) * rows, 8), rows), :] = pair_tmp[pl.ds(h * rows, rows), :]
            w[2 * c + h, z, x] = tmp[...].astype(bf16)
            gather_copy(2 * c + h, h, 0).start()
            gather_copy(2 * c + h, h, 1).start()

    def gather_forward(k):
        def step(u, p):
            gather_copy(u, p, k).wait_recv()
            gather_copy(u, p, k + 2).start()
            gather_copy(u, p, k + 1).wait_recv()
            gather_copy(u, p, k + 3).start()
        return both(step)

    @both
    def gather_second(u, p):
        gather_copy(u, p, 2).wait_recv()
        gather_copy(u, p, 3).wait_recv()
        gather_copy(u, p, 4).start()
        gather_copy(u, p, 5).start()

    @both
    def gather_end(u, p):
        gather_copy(u, p, 6).wait_recv()
        gather_copy(u, p, 7).wait_recv()

    def own_hidden(c):
        gather_end(c)
        own_cot(c).wait()
        hidden(c, 0)

    def add_into(ref, other):
        ref[...] = (ref[...].astype(f32) + other[...].astype(f32)).astype(bf16)

    def back_part(n, start, units):
        part = jnp.concatenate(
            [w[u, pl.ds(2 * n, 2)].reshape(bk_cols, LANES) for u in units], axis=1
        )
        cols = slice(units[0] * LANES, (units[-1] + 1) * LANES)
        return lax.dot_general(
            cb[pl.ds(start, tok), cols], part, (((1,), (1,)), ((), ())), preferred_element_type=f32
        )

    def send_back(n, term):
        for m in range(n_bk // 2):
            i = n * (n_bk // 2) + m
            bks[i] = term[m * bk_rows : (m + 1) * bk_rows].astype(bf16)
            bk_copy(i).start()

    middle = n_chunks // 2
    early = range(2 * middle)
    late = range(2 * middle, 2 * n_chunks - 2)
    final = range(2 * n_chunks - 2, 2 * n_chunks)

    def work(c):
        @pl.when(c == middle)
        def _():
            acc[0] = back_part(0, tok, early)

        @pl.when(c == n_chunks - 1)
        def _():
            d_copy(1).start()
            acc[0] = acc[0] + back_part(0, tok, late)

        cot_copy(c).wait_recv()

        @pl.when(c + ahead < n_chunks)
        def _():
            cot_copy(c + ahead).start()

        hidden(c, tok)

        @pl.when(c == n_chunks - 1)
        def _():
            send_back(0, acc[0] + back_part(0, tok, final))

        term = lax.dot_general(
            xb[...], cb[:, chunk_cols(c)], (((0,), (0,)), ((), ())), preferred_element_type=f32
        ).astype(bf16)
        for h in range(2):
            g[2 * c + h] = term[:, h * LANES : (h + 1) * LANES].reshape(4, 4, block, LANES)
        for p in range(2):
            scatter_copy(2 * c + p, p, 0).start()
            scatter_copy(2 * c + p, p, 1).start()

    @both
    def scatter_second(u, p):
        b = second_axis[p]
        scatter_copy(u, p, 0).wait_recv()
        add_into(half2(g, u, p, after[b], 0), rah.at[u, 0])
        scatter_copy(u, p, 2).start()
        scatter_copy(u, p, 1).wait_recv()
        add_into(half2(g, u, p, before[b], 1), rah.at[u, 1])
        scatter_copy(u, p, 3).start()

    @both
    def scatter_third(u, p):
        b = second_axis[p]
        scatter_copy(u, p, 2).wait_recv()
        scatter_copy(u, p, 3).wait_recv()
        mine = seg2(g, u, p, place[b])
        mine[...] = (
            mine[...].astype(f32) + raf[u, 0].astype(f32) + raf[u, 1].astype(f32)
        ).astype(bf16)
        scatter_copy(u, p, 4).start()
        scatter_copy(u, p, 5).start()

    @both
    def scatter_fourth(u, p):
        a = first_axis[p]
        scatter_copy(u, p, 4).wait_recv()
        add_into(half1(g, u, p, after[a], 0), rbh.at[u, pl.ds(0, cut)])
        scatter_copy(u, p, 6).start()
        scatter_copy(u, p, 5).wait_recv()
        add_into(half1(g, u, p, before[a], 1), rbh.at[u, pl.ds(cut, block - cut)])
        scatter_copy(u, p, 7).start()

    @both
    def scatter_end(u, p):
        a = first_axis[p]
        for k in range(6):
            scatter_copy(u, p, k).wait_send()
        scatter_copy(u, p, 6).wait_recv()
        scatter_copy(u, p, 7).wait_recv()
        mine = seg1(g, u, p, place[a])
        tmp[...] = mine[...].astype(f32) + rbf[u, 0].astype(f32) + rbf[u, 1].astype(f32)
        pair_tmp[pl.ds(p * rows, rows), :] = tmp[pl.ds(pl.multiple_of((1 - yh) * rows, 8), rows), :]
        cols = pl.ds(pl.multiple_of(my_base + u * LANES, LANES), LANES)
        g_ref[:, cols] = tmp[pl.ds(pl.multiple_of(yh * rows, 8), rows), :]
        if p == 1:
            c = lax.div(u, 2)
            gps[c] = pair_tmp[...].astype(bf16)
            gp_copy(c).start()
            g_out(c, my_base, 0).start()

    def keep_back(n):
        acc[n] = back_part(n, 0, range(2 * n_chunks))

    def settle(c):
        pw_copy(c).wait_send()
        cot_copy(c).wait_send()
        for p in range(2):
            for k in range(8):
                gather_copy(2 * c + p, p, k).wait_send()

    def tick(t):
        ranged(t, 0, gather_own)
        ranged(t, 1, gather_forward(0))
        ranged(t, 2, gather_second)
        ranged(t, 3, gather_forward(4))

        @pl.when(t == 4)
        def _():
            own_x().wait()

        ranged(t, 4, own_hidden)

        @pl.when(t == 1)
        def _():
            d_copy(0).wait_recv()
            ds[1] = (ds[0].astype(f32) + dr[0].astype(f32)).astype(bf16)

        @pl.when(t == 8)
        def _():
            for c in range(ahead):
                cot_copy(c).start()

        @pl.when(t == work_lag)
        def _():
            for i in range(n_x):
                x_copy(i).wait_recv()

        ranged(t, work_lag, work)

        @pl.when(t == done)
        def _():
            send_back(1, back_part(1, tok, range(2 * n_chunks)))

        @pl.when((t >= done + 1) & (t < done + 3))
        def _():
            keep_back(t - done - 1)

        ranged(t, work_lag + 2, settle)
        ranged(t, work_lag + 3, scatter_second)
        ranged(t, work_lag + 6, scatter_third)
        ranged(t, work_lag + 8, scatter_fourth)
        ranged(t, work_lag + 9, scatter_end)

    each(n_chunks + work_lag + 9, tick)

    def finish_back(i):
        bk_copy(i).wait_recv()
        n, m = lax.div(i, n_bk // 2), lax.rem(i, n_bk // 2)
        at = pl.ds(pl.multiple_of(m * bk_rows, 16), bk_rows)
        cols = pl.ds(pl.multiple_of(n * bk_cols, LANES), bk_cols)
        out_ref[at, cols] = (acc[n, at, :] + bkr[i].astype(f32)).astype(bf16)
        back_out(i).start()

    d_copy(1).wait_recv()
    total_ref[...] = (ds[1].astype(f32) + dr[1].astype(f32))[:rows]
    total_out().start()

    def finish_grad(c):
        gp_copy(c).wait_recv()
        pair_tmp[...] = gpr[c].astype(f32)
        for h in range(2):
            cols = pl.ds(pl.multiple_of(peer_base + c * CHUNK + h * LANES, LANES), LANES)
            g_ref[:, cols] = pair_tmp[pl.ds(h * rows, rows), :]
        g_out(c, peer_base, 1).start()

    each(n_bk, finish_back)
    each(n_chunks, finish_grad)

    def finish(c):
        gp_copy(c).wait_send()
        for p in range(2):
            for k in range(6, 8):
                scatter_copy(2 * c + p, p, k).wait_send()
        g_out(c, my_base, 0).wait()
        g_out(c, peer_base, 1).wait()

    each(n_chunks, finish)
    each(n_x, lambda i: x_copy(i).wait_send())
    for i in range(2):
        d_copy(i).wait_send()
    total_out().wait()

    def finish_out(i):
        bk_copy(i).wait_send()
        back_out(i).wait()

    each(n_bk, finish_out)


def projection(fragment, acts, cot, weights, snapshot):
    tok, width = acts.shape
    rows, ffw = weights.shape
    frag = snapshot.shape[1]
    units = ffw // 2 // LANES
    chunks = units // 2
    block = 2 * rows
    pad_rows = (rows + 15) // 16 * 16
    n_x, n_bk = 3, 6
    dma = pltpu.SemaphoreType.DMA
    vmem = pltpu.VMEM
    return pl.pallas_call(
        pair_kernel,
        out_shape=(
            jax.ShapeDtypeStruct((tok, width), bf16),
            jax.ShapeDtypeStruct((rows, ffw), f32),
            jax.ShapeDtypeStruct((rows, frag), f32),
        ),
        in_specs=[
            pl.BlockSpec(memory_space=pltpu.SMEM),
            pl.BlockSpec(memory_space=pl.ANY),
            pl.BlockSpec(memory_space=pl.ANY),
            pl.BlockSpec(memory_space=pl.ANY),
            pl.BlockSpec(memory_space=pl.ANY),
        ],
        out_specs=(
            pl.BlockSpec(memory_space=pl.ANY),
            pl.BlockSpec(memory_space=pl.ANY),
            pl.BlockSpec(memory_space=pl.ANY),
        ),
        scratch_shapes=[
            vmem((rows, ffw), f32),
            vmem((rows, frag), f32),
            vmem((tok, width), bf16),
            vmem((rows, ffw), f32),
            vmem((rows, frag), f32),
            vmem((2 * tok, width), bf16),
            vmem((2 * tok, ffw // 2), bf16),
            vmem((units, 4, 4, block, LANES), bf16),
            vmem((units, 4, 4, block, LANES), bf16),
            vmem((units, 2, 2, block, LANES), bf16),
            vmem((units, 2, 4, block, LANES), bf16),
            vmem((units, block, LANES), bf16),
            vmem((units, 2, block, LANES), bf16),
            vmem((chunks, block, LANES), bf16),
            vmem((chunks, block, LANES), bf16),
            vmem((chunks, block, LANES), bf16),
            vmem((chunks, block, LANES), bf16),
            vmem((n_bk, tok // (n_bk // 2), width // 2), bf16),
            vmem((n_bk, tok // (n_bk // 2), width // 2), bf16),
            vmem((block, LANES), f32),
            vmem((2, tok, width // 2), f32),
            vmem((block, LANES), f32),
            vmem((2, pad_rows, frag), bf16),
            vmem((2, pad_rows, frag), bf16),
            dma((chunks + 3,)),
            dma((units, 8)), dma((units, 8)),
            dma((units, 8)), dma((units, 8)),
            dma((chunks,)), dma((chunks,)),
            dma((n_x,)), dma((n_x,)),
            dma((chunks,)), dma((chunks,)),
            dma((n_bk,)), dma((n_bk,)),
            dma((chunks,)), dma((chunks,)),
            dma((2,)), dma((2,)),
            dma((n_bk,)), dma((units,)), dma((1,)),
        ],
        compiler_params=pltpu.CompilerParams(
            collective_id=1, has_side_effects=True, vmem_limit_bytes=60 * 2**20
        ),
        cost_estimate=pl.CostEstimate(
            flops=6 * tok * width * ffw, bytes_accessed=16 * tok * width, transcendentals=tok * ffw
        ),
        name="pair_projection",
    )(fragment, acts, cot, weights, snapshot)


def update_kernel(
    frag_ref, g_ref, p_ref, m_ref, v_ref, snap_ref, mom_ref, total_ref, back_hbm,
    new_p, new_m, new_v, new_mom, new_snap, out_hbm, sem,
):
    pass_on = pltpu.make_async_copy(back_hbm, out_hbm, sem)
    pass_on.start()
    frag = snap_ref.shape[1]
    outer = total_ref[...] * 0.25
    mom = outer_mu * mom_ref[...] + outer
    new_mom[...] = mom
    snap = snap_ref[...] - outer_rate * (outer + outer_mu * mom)
    new_snap[...] = snap
    grad = g_ref[...]
    weights = p_ref[...]
    first = beta_one * m_ref[...] + (1.0 - beta_one) * grad
    second = beta_two * v_ref[...] + (1.0 - beta_two) * grad * grad
    new_m[...] = first
    new_v[...] = second
    new_p[...] = weights - inner_rate * (
        first / (jnp.sqrt(second) + adam_eps) + decay_rate * weights
    )
    at = pl.ds(pl.multiple_of(frag_ref[0] * frag, LANES), frag)
    new_p[:, at] = mix_rate * snap + (1.0 - mix_rate) * new_p[:, at]
    pass_on.wait()


def update(fragment, grad, weights, first, second, snapshot, momentum, total, back):
    full = jax.ShapeDtypeStruct(weights.shape, f32)
    part = jax.ShapeDtypeStruct(snapshot.shape, f32)
    vmem = pl.BlockSpec(memory_space=pltpu.VMEM)
    hbm = pl.BlockSpec(memory_space=pl.ANY)
    return pl.pallas_call(
        update_kernel,
        in_specs=[pl.BlockSpec(memory_space=pltpu.SMEM)] + [vmem] * 7 + [hbm],
        out_specs=[vmem] * 5 + [hbm],
        out_shape=[full] * 3 + [part] * 2 + [jax.ShapeDtypeStruct(back.shape, back.dtype)],
        scratch_shapes=[pltpu.SemaphoreType.DMA],
        compiler_params=pltpu.CompilerParams(vmem_limit_bytes=60 * 2**20),
        name="update",
    )(fragment, grad, weights, first, second, snapshot, momentum, total, back)


def body(inputs, cotangent, params, first_moment, second_moment, snapshot, momentum, fragment):
    back, grad, total = projection(fragment, inputs[0], cotangent[0], params[0], snapshot)
    stepped, first, second, new_momentum, new_snapshot, input_grad = update(
        fragment, grad, params[0], first_moment[0], second_moment[0], snapshot, momentum, total, back
    )
    return (stepped[None], first[None], second[None], input_grad[None], new_momentum, new_snapshot)


def solution(mesh):
    return jax.shard_map(
        body,
        mesh=mesh,
        in_specs=(
            P("rep", "fsdp", None),
            P("rep", "fsdp", None),
            P("rep", "fsdp", None),
            P("rep", "fsdp", None),
            P("rep", "fsdp", None),
            P("fsdp", None),
            P("fsdp", None),
            P(),
        ),
        out_specs=(
            P("rep", "fsdp", None),
            P("rep", "fsdp", None),
            P("rep", "fsdp", None),
            P("rep", "fsdp", None),
            P("fsdp", None),
            P("fsdp", None),
        ),
        check_vma=False,
    )
```

```python
import functools

import jax
import jax.numpy as jnp
from jax import lax
from jax.experimental import pallas as pl
from jax.experimental.pallas import tpu as pltpu
from jax.sharding import PartitionSpec as P

beta_one = 0.9
beta_two = 0.95
inner_rate = 0.01
adam_eps = 1e-08
decay_rate = 0.1
outer_rate = 0.7
outer_mu = 0.9
mix_rate = 0.5

LANES = 128
CHUNK = 256
MESH = pl.DeviceIdType.MESH
f32 = jnp.float32
bf16 = jnp.bfloat16


def gelu_slope(t):
    c = 0.7978845608028654
    sq = t * t
    th = jnp.tanh(c * t * (1.0 + 0.044715 * sq))
    return 0.5 * (1.0 + th) + 0.5 * t * (1.0 - th * th) * (c * (1.0 + 3 * 0.044715 * sq))


def pair_kernel(
    frag_ref, x_hbm, cot_hbm, p_hbm, snap_hbm,
    out_hbm, g_hbm, total_hbm,
    p_ref, snap_ref, out_ref, g_ref, total_ref,
    xb, cb, w, g, rah, raf, rbh, rbf, pws, pwr, gps, gpr, bks, bkr, tmp, acc, pair_tmp, ds, dr, dq, dt, du,
    loc_sem, ag_send, ag_recv, rs_send, rs_recv, pw_send, pw_recv,
    x_send, x_recv, cot_send, cot_recv, bk_send, bk_recv, gp_send, gp_recv, d_send, d_recv,
    out_sem, g_sem, total_sem,
):
    tok, width = x_hbm.shape
    rows, ffw = p_ref.shape
    half_cols = ffw // 2
    n_chunks = half_cols // CHUNK
    block = 2 * rows
    pad_rows = ds.shape[1]
    part_rows = dq.shape[0]
    core = lax.rem(lax.axis_index("rep"), 2)
    part = pl.ds(pl.multiple_of(core * (pad_rows - part_rows), 16), part_rows)
    frag = snap_ref.shape[1]
    cut = (block // 16 + 1) // 2 * 16
    n_x = x_send.shape[0]
    x_rows = tok // n_x
    n_bk = bk_send.shape[0]
    bk_rows = tok // (n_bk // 2)
    bk_cols = width // 2
    scale = width ** (-0.5)
    ahead = 6
    work_lag = 10
    done = work_lag + n_chunks

    f = lax.axis_index("fsdp")
    r = lax.axis_index("rep")
    yh = lax.rem(f, 2)
    x = lax.rem(lax.div(f, 2), 4)
    z = lax.div(f, 8)

    def device(zz, xx, yy):
        return {"fsdp": zz * 8 + xx * 2 + yy}

    peer = device(z, x, 1 - yh)
    sibling = {"rep": r + 1 - 2 * lax.rem(r, 2)}
    neighbour = {"rep": lax.rem(r + 2, 4)}
    place = {"x": x, "z": z}
    after = {a: lax.rem(place[a] + 1, 4) for a in place}
    before = {a: lax.rem(place[a] + 3, 4) for a in place}
    across = {a: lax.rem(place[a] + 2, 4) for a in place}
    right = {"x": device(z, after["x"], yh), "z": device(after["z"], x, yh)}
    left = {"x": device(z, before["x"], yh), "z": device(before["z"], x, yh)}
    first_axis = ("x", "z")
    second_axis = ("z", "x")
    my_base = yh * half_cols
    peer_base = (1 - yh) * half_cols

    def seg2(ref, u, p, i):
        return ref.at[u, i] if p == 0 else ref.at[u, :, i]

    def half2(ref, u, p, i, h):
        part = pl.ds(2 * h, 2)
        return ref.at[u, i, part] if p == 0 else ref.at[u, part, i]

    def seg1(ref, u, p, i):
        return ref.at[u, z, i] if p == 0 else ref.at[u, i, x]

    def half1(ref, u, p, i, h):
        part = pl.ds(0, cut) if h == 0 else pl.ds(cut, block - cut)
        return ref.at[u, z, i, part] if p == 0 else ref.at[u, i, x, part]

    def chunk_cols(c):
        return pl.ds(pl.multiple_of(c * CHUNK, CHUNK), CHUNK)

    def remote(src, dst, send, recv, to):
        return pltpu.make_async_remote_copy(
            src_ref=src, dst_ref=dst, send_sem=send, recv_sem=recv, device_id=to, device_id_type=MESH
        )

    def gather_copy(u, p, k):
        a, b = first_axis[p], second_axis[p]
        part = (
            lambda: seg1(w, u, p, place[a]),
            lambda: seg1(w, u, p, place[a]),
            lambda: half1(w, u, p, before[a], 0),
            lambda: half1(w, u, p, after[a], 1),
            lambda: seg2(w, u, p, place[b]),
            lambda: seg2(w, u, p, place[b]),
            lambda: half2(w, u, p, before[b], 0),
            lambda: half2(w, u, p, after[b], 1),
        )[k]()
        to = (right if k % 2 == 0 else left)[a if k < 4 else b]
        return remote(part, part, ag_send.at[u, k], ag_recv.at[u, k], to)

    def scatter_copy(u, p, k):
        a, b = first_axis[p], second_axis[p]
        src, dst = (
            lambda: (half2(g, u, p, across[b], 0), rah.at[u, 0]),
            lambda: (half2(g, u, p, across[b], 1), rah.at[u, 1]),
            lambda: (seg2(g, u, p, after[b]), raf.at[u, 0]),
            lambda: (seg2(g, u, p, before[b]), raf.at[u, 1]),
            lambda: (half1(g, u, p, across[a], 0), rbh.at[u, pl.ds(0, cut)]),
            lambda: (half1(g, u, p, across[a], 1), rbh.at[u, pl.ds(cut, block - cut)]),
            lambda: (seg1(g, u, p, after[a]), rbf.at[u, 0]),
            lambda: (seg1(g, u, p, before[a]), rbf.at[u, 1]),
        )[k]()
        to = (right if k % 2 == 0 else left)[b if k < 4 else a]
        return remote(src, dst, rs_send.at[u, k], rs_recv.at[u, k], to)

    def pw_copy(c):
        return remote(pws.at[c], pwr.at[c], pw_send.at[c], pw_recv.at[c], peer)

    def x_copy(i):
        return remote(
            x_hbm.at[pl.ds(i * x_rows, x_rows)], xb.at[pl.ds(tok + i * x_rows, x_rows)],
            x_send.at[i], x_recv.at[i], peer,
        )

    def cot_copy(c):
        cols = pl.ds(pl.multiple_of(peer_base + c * CHUNK, CHUNK), CHUNK)
        return remote(
            cot_hbm.at[:, cols], cb.at[pl.ds(tok, tok), chunk_cols(c)],
            cot_send.at[c], cot_recv.at[c], peer,
        )

    def bk_copy(i):
        return remote(bks.at[i], bkr.at[i], bk_send.at[i], bk_recv.at[i], peer)

    def gp_copy(c):
        return remote(gps.at[c], gpr.at[c], gp_send.at[c], gp_recv.at[c], peer)

    def g_out(c, base, h):
        cols = pl.ds(pl.multiple_of(base + c * CHUNK, CHUNK), CHUNK)
        return pltpu.make_async_copy(g_ref.at[:, cols], g_hbm.at[:, cols], g_sem.at[2 * c + h])

    def total_out():
        return pltpu.make_async_copy(total_ref, total_hbm, total_sem.at[0])

    def back_out(i):
        n, m = lax.div(i, n_bk // 2), lax.rem(i, n_bk // 2)
        at = pl.ds(pl.multiple_of(m * bk_rows, 16), bk_rows)
        cols = pl.ds(pl.multiple_of(n * bk_cols, LANES), bk_cols)
        return pltpu.make_async_copy(out_ref.at[at, cols], out_hbm.at[at, cols], out_sem.at[i])

    def d_copy(i):
        src, dst, to = (
            (ds.at[0], dr, sibling),
            (ds.at[1, part], dq, neighbour),
            (dt, du, sibling),
        )[i]
        return remote(src, dst, d_send.at[i], d_recv.at[i], to)

    def own_x():
        return pltpu.make_async_copy(x_hbm, xb.at[pl.ds(0, tok)], loc_sem.at[n_chunks])

    def own_params():
        return pltpu.make_async_copy(p_hbm, p_ref, loc_sem.at[n_chunks + 1])

    def own_snap():
        return pltpu.make_async_copy(snap_hbm, snap_ref, loc_sem.at[n_chunks + 2])

    def own_cot(c):
        cols = pl.ds(pl.multiple_of(my_base + c * CHUNK, CHUNK), CHUNK)
        return pltpu.make_async_copy(
            cot_hbm.at[:, cols], cb.at[pl.ds(0, tok), chunk_cols(c)], loc_sem.at[c]
        )

    def each(count, step):
        def run(i, carry):
            step(i)
            return carry
        lax.fori_loop(0, count, run, 0)

    def ranged(t, lag, step):
        @pl.when((t >= lag) & (t < lag + n_chunks))
        def _():
            step(t - lag)

    def both(step):
        def run(c):
            for p in range(2):
                step(2 * c + p, p)
        return run

    barrier = pltpu.get_barrier_semaphore()
    partners = (peer, right["x"], left["x"], right["z"], left["z"], sibling, neighbour)
    for partner in partners:
        pl.semaphore_signal(barrier, inc=1, device_id=partner, device_id_type=MESH)
    own_params().start()
    own_snap().start()
    own_x().start()
    each(n_chunks, lambda c: own_cot(c).start())
    own_params().wait()
    pl.semaphore_wait(barrier, len(partners))

    def prepare(c):
        parts = []
        for h in range(2):
            cols = pl.ds(pl.multiple_of(peer_base + c * CHUNK + h * LANES, LANES), LANES)
            parts.append(p_ref[:, cols])
        pws[c] = jnp.concatenate(parts, axis=0).astype(bf16)
        pw_copy(c).start()

    each(n_chunks, prepare)
    each(n_x, lambda i: x_copy(i).start())
    own_snap().wait()
    local = p_ref[:, :frag]
    for i in range(1, ffw // frag):
        local = jnp.where(frag_ref[0] == i, p_ref[:, i * frag : (i + 1) * frag], local)
    delta = snap_ref[...] - local
    ds[0] = jnp.concatenate([delta, jnp.zeros((pad_rows - rows, frag), f32)], axis=0).astype(bf16)

    d_copy(0).start()

    def chunk_weights(c):
        return jnp.concatenate(
            [w[2 * c].reshape(width, LANES), w[2 * c + 1].reshape(width, LANES)], axis=1
        )

    def hidden(c, start):
        at = pl.ds(start, tok)
        pre = jnp.dot(xb[at, :], chunk_weights(c), preferred_element_type=f32) * scale
        cot = cb[at, chunk_cols(c)].astype(f32)
        cb[at, chunk_cols(c)] = (gelu_slope(pre) * cot * scale).astype(bf16)

    def gather_own(c):
        pw_copy(c).wait_recv()
        pair_tmp[...] = pwr[c].astype(f32)
        for h in range(2):
            cols = pl.ds(pl.multiple_of(my_base + c * CHUNK + h * LANES, LANES), LANES)
            tmp[pl.ds(pl.multiple_of(yh * rows, 8), rows), :] = p_ref[:, cols]
            tmp[pl.ds(pl.multiple_of((1 - yh) * rows, 8), rows), :] = pair_tmp[pl.ds(h * rows, rows), :]
            w[2 * c + h, z, x] = tmp[...].astype(bf16)
            gather_copy(2 * c + h, h, 0).start()
            gather_copy(2 * c + h, h, 1).start()

    def gather_forward(k):
        def step(u, p):
            gather_copy(u, p, k).wait_recv()
            gather_copy(u, p, k + 2).start()
            gather_copy(u, p, k + 1).wait_recv()
            gather_copy(u, p, k + 3).start()
        return both(step)

    @both
    def gather_second(u, p):
        gather_copy(u, p, 2).wait_recv()
        gather_copy(u, p, 3).wait_recv()
        gather_copy(u, p, 4).start()
        gather_copy(u, p, 5).start()

    @both
    def gather_end(u, p):
        gather_copy(u, p, 6).wait_recv()
        gather_copy(u, p, 7).wait_recv()

    def own_hidden(c):
        gather_end(c)
        own_cot(c).wait()
        hidden(c, 0)

    def add_into(ref, other):
        ref[...] = (ref[...].astype(f32) + other[...].astype(f32)).astype(bf16)

    def back_part(n, start, units):
        part = jnp.concatenate(
            [w[u, pl.ds(2 * n, 2)].reshape(bk_cols, LANES) for u in units], axis=1
        )
        cols = slice(units[0] * LANES, (units[-1] + 1) * LANES)
        return lax.dot_general(
            cb[pl.ds(start, tok), cols], part, (((1,), (1,)), ((), ())), preferred_element_type=f32
        )

    def send_back(n, term):
        for m in range(n_bk // 2):
            i = n * (n_bk // 2) + m
            bks[i] = term[m * bk_rows : (m + 1) * bk_rows].astype(bf16)
            bk_copy(i).start()

    middle = n_chunks // 2
    early = range(2 * middle)
    late = range(2 * middle, 2 * n_chunks - 2)
    final = range(2 * n_chunks - 2, 2 * n_chunks)

    def work(c):
        @pl.when(c == middle)
        def _():
            acc[0] = back_part(0, tok, early)

        @pl.when(c == n_chunks - 1)
        def _():
            d_copy(1).start()
            acc[0] = acc[0] + back_part(0, tok, late)

        cot_copy(c).wait_recv()

        @pl.when(c + ahead < n_chunks)
        def _():
            cot_copy(c + ahead).start()

        hidden(c, tok)

        @pl.when(c == n_chunks - 1)
        def _():
            send_back(0, acc[0] + back_part(0, tok, final))

        term = lax.dot_general(
            xb[...], cb[:, chunk_cols(c)], (((0,), (0,)), ((), ())), preferred_element_type=f32
        ).astype(bf16)
        for h in range(2):
            g[2 * c + h] = term[:, h * LANES : (h + 1) * LANES].reshape(4, 4, block, LANES)
        for p in range(2):
            scatter_copy(2 * c + p, p, 0).start()
            scatter_copy(2 * c + p, p, 1).start()

    @both
    def scatter_second(u, p):
        b = second_axis[p]
        scatter_copy(u, p, 0).wait_recv()
        add_into(half2(g, u, p, after[b], 0), rah.at[u, 0])
        scatter_copy(u, p, 2).start()
        scatter_copy(u, p, 1).wait_recv()
        add_into(half2(g, u, p, before[b], 1), rah.at[u, 1])
        scatter_copy(u, p, 3).start()

    @both
    def scatter_third(u, p):
        b = second_axis[p]
        scatter_copy(u, p, 2).wait_recv()
        scatter_copy(u, p, 3).wait_recv()
        mine = seg2(g, u, p, place[b])
        mine[...] = (
            mine[...].astype(f32) + raf[u, 0].astype(f32) + raf[u, 1].astype(f32)
        ).astype(bf16)
        scatter_copy(u, p, 4).start()
        scatter_copy(u, p, 5).start()

    @both
    def scatter_fourth(u, p):
        a = first_axis[p]
        scatter_copy(u, p, 4).wait_recv()
        add_into(half1(g, u, p, after[a], 0), rbh.at[u, pl.ds(0, cut)])
        scatter_copy(u, p, 6).start()
        scatter_copy(u, p, 5).wait_recv()
        add_into(half1(g, u, p, before[a], 1), rbh.at[u, pl.ds(cut, block - cut)])
        scatter_copy(u, p, 7).start()

    @both
    def scatter_end(u, p):
        a = first_axis[p]
        for k in range(6):
            scatter_copy(u, p, k).wait_send()
        scatter_copy(u, p, 6).wait_recv()
        scatter_copy(u, p, 7).wait_recv()
        mine = seg1(g, u, p, place[a])
        tmp[...] = mine[...].astype(f32) + rbf[u, 0].astype(f32) + rbf[u, 1].astype(f32)
        pair_tmp[pl.ds(p * rows, rows), :] = tmp[pl.ds(pl.multiple_of((1 - yh) * rows, 8), rows), :]
        cols = pl.ds(pl.multiple_of(my_base + u * LANES, LANES), LANES)
        g_ref[:, cols] = tmp[pl.ds(pl.multiple_of(yh * rows, 8), rows), :]
        if p == 1:
            c = lax.div(u, 2)
            gps[c] = pair_tmp[...].astype(bf16)
            gp_copy(c).start()
            g_out(c, my_base, 0).start()

    def keep_back(n):
        acc[n] = back_part(n, 0, range(2 * n_chunks))

    def settle(c):
        pw_copy(c).wait_send()
        cot_copy(c).wait_send()
        for p in range(2):
            for k in range(8):
                gather_copy(2 * c + p, p, k).wait_send()

    def tick(t):
        ranged(t, 0, gather_own)
        ranged(t, 1, gather_forward(0))
        ranged(t, 2, gather_second)
        ranged(t, 3, gather_forward(4))

        @pl.when(t == 4)
        def _():
            own_x().wait()

        ranged(t, 4, own_hidden)

        @pl.when(t == 1)
        def _():
            d_copy(0).wait_recv()
            ds[1] = (ds[0].astype(f32) + dr[...].astype(f32)).astype(bf16)

        @pl.when(t == 8)
        def _():
            for c in range(ahead):
                cot_copy(c).start()

        @pl.when(t == work_lag)
        def _():
            for i in range(n_x):
                x_copy(i).wait_recv()

        ranged(t, work_lag, work)

        @pl.when(t == done)
        def _():
            send_back(1, back_part(1, tok, range(2 * n_chunks)))

        @pl.when((t >= done + 1) & (t < done + 3))
        def _():
            keep_back(t - done - 1)

        ranged(t, work_lag + 2, settle)
        ranged(t, work_lag + 3, scatter_second)
        ranged(t, work_lag + 6, scatter_third)
        ranged(t, work_lag + 8, scatter_fourth)
        ranged(t, work_lag + 9, scatter_end)

    each(n_chunks + work_lag + 9, tick)

    def finish_back(i):
        bk_copy(i).wait_recv()
        n, m = lax.div(i, n_bk // 2), lax.rem(i, n_bk // 2)
        at = pl.ds(pl.multiple_of(m * bk_rows, 16), bk_rows)
        cols = pl.ds(pl.multiple_of(n * bk_cols, LANES), bk_cols)
        out_ref[at, cols] = (acc[n, at, :] + bkr[i].astype(f32)).astype(bf16)
        back_out(i).start()


    def finish_grad(c):
        gp_copy(c).wait_recv()
        pair_tmp[...] = gpr[c].astype(f32)
        for h in range(2):
            cols = pl.ds(pl.multiple_of(peer_base + c * CHUNK + h * LANES, LANES), LANES)
            g_ref[:, cols] = pair_tmp[pl.ds(h * rows, rows), :]
        g_out(c, peer_base, 1).start()

    d_copy(1).wait_recv()
    dt[...] = ds[1, part].astype(f32) + dq[...].astype(f32)
    d_copy(2).start()
    each(n_bk, finish_back)
    d_copy(2).wait_recv()
    total_ref[...] = jnp.where(
        core == 0,
        jnp.concatenate([dt[...], du[2 * part_rows - pad_rows :]], axis=0)[:rows],
        jnp.concatenate([du[...], dt[2 * part_rows - pad_rows :]], axis=0)[:rows],
    )
    total_out().start()
    each(n_chunks, finish_grad)

    def finish(c):
        gp_copy(c).wait_send()
        for p in range(2):
            for k in range(6, 8):
                scatter_copy(2 * c + p, p, k).wait_send()
        g_out(c, my_base, 0).wait()
        g_out(c, peer_base, 1).wait()

    each(n_chunks, finish)
    each(n_x, lambda i: x_copy(i).wait_send())
    for i in range(3):
        d_copy(i).wait_send()
    total_out().wait()

    def finish_out(i):
        bk_copy(i).wait_send()
        back_out(i).wait()

    each(n_bk, finish_out)


def projection(fragment, acts, cot, weights, snapshot):
    tok, width = acts.shape
    rows, ffw = weights.shape
    frag = snapshot.shape[1]
    units = ffw // 2 // LANES
    chunks = units // 2
    block = 2 * rows
    pad_rows = (rows + 15) // 16 * 16
    part_rows = (pad_rows // 16 + 1) // 2 * 16
    n_x, n_bk = 3, 6
    dma = pltpu.SemaphoreType.DMA
    vmem = pltpu.VMEM
    return pl.pallas_call(
        pair_kernel,
        out_shape=(
            jax.ShapeDtypeStruct((tok, width), bf16),
            jax.ShapeDtypeStruct((rows, ffw), f32),
            jax.ShapeDtypeStruct((rows, frag), f32),
        ),
        in_specs=[
            pl.BlockSpec(memory_space=pltpu.SMEM),
            pl.BlockSpec(memory_space=pl.ANY),
            pl.BlockSpec(memory_space=pl.ANY),
            pl.BlockSpec(memory_space=pl.ANY),
            pl.BlockSpec(memory_space=pl.ANY),
        ],
        out_specs=(
            pl.BlockSpec(memory_space=pl.ANY),
            pl.BlockSpec(memory_space=pl.ANY),
            pl.BlockSpec(memory_space=pl.ANY),
        ),
        scratch_shapes=[
            vmem((rows, ffw), f32),
            vmem((rows, frag), f32),
            vmem((tok, width), bf16),
            vmem((rows, ffw), f32),
            vmem((rows, frag), f32),
            vmem((2 * tok, width), bf16),
            vmem((2 * tok, ffw // 2), bf16),
            vmem((units, 4, 4, block, LANES), bf16),
            vmem((units, 4, 4, block, LANES), bf16),
            vmem((units, 2, 2, block, LANES), bf16),
            vmem((units, 2, 4, block, LANES), bf16),
            vmem((units, block, LANES), bf16),
            vmem((units, 2, block, LANES), bf16),
            vmem((chunks, block, LANES), bf16),
            vmem((chunks, block, LANES), bf16),
            vmem((chunks, block, LANES), bf16),
            vmem((chunks, block, LANES), bf16),
            vmem((n_bk, tok // (n_bk // 2), width // 2), bf16),
            vmem((n_bk, tok // (n_bk // 2), width // 2), bf16),
            vmem((block, LANES), f32),
            vmem((2, tok, width // 2), f32),
            vmem((block, LANES), f32),
            vmem((2, pad_rows, frag), bf16),
            vmem((pad_rows, frag), bf16),
            vmem((part_rows, frag), bf16),
            vmem((part_rows, frag), f32),
            vmem((part_rows, frag), f32),
            dma((chunks + 3,)),
            dma((units, 8)), dma((units, 8)),
            dma((units, 8)), dma((units, 8)),
            dma((chunks,)), dma((chunks,)),
            dma((n_x,)), dma((n_x,)),
            dma((chunks,)), dma((chunks,)),
            dma((n_bk,)), dma((n_bk,)),
            dma((chunks,)), dma((chunks,)),
            dma((3,)), dma((3,)),
            dma((n_bk,)), dma((units,)), dma((1,)),
        ],
        compiler_params=pltpu.CompilerParams(
            collective_id=1, has_side_effects=True, vmem_limit_bytes=60 * 2**20
        ),
        cost_estimate=pl.CostEstimate(
            flops=6 * tok * width * ffw, bytes_accessed=16 * tok * width, transcendentals=tok * ffw
        ),
        name="pair_projection",
    )(fragment, acts, cot, weights, snapshot)


def update_kernel(
    frag_ref, g_ref, p_ref, m_ref, v_ref, snap_ref, mom_ref, total_ref, back_hbm,
    new_p, new_m, new_v, new_mom, new_snap, out_hbm, held, sem,
):
    bring = pltpu.make_async_copy(back_hbm, held, sem.at[0])
    pass_on = pltpu.make_async_copy(held, out_hbm, sem.at[1])
    bring.start()
    frag = snap_ref.shape[1]
    outer = total_ref[...] * 0.25
    mom = outer_mu * mom_ref[...] + outer
    new_mom[...] = mom
    snap = snap_ref[...] - outer_rate * (outer + outer_mu * mom)
    new_snap[...] = snap
    bring.wait()
    pass_on.start()
    grad = g_ref[...]
    weights = p_ref[...]
    first = beta_one * m_ref[...] + (1.0 - beta_one) * grad
    second = beta_two * v_ref[...] + (1.0 - beta_two) * grad * grad
    new_m[...] = first
    new_v[...] = second
    new_p[...] = weights - inner_rate * (
        first / (jnp.sqrt(second) + adam_eps) + decay_rate * weights
    )
    at = pl.ds(pl.multiple_of(frag_ref[0] * frag, LANES), frag)
    new_p[:, at] = mix_rate * snap + (1.0 - mix_rate) * new_p[:, at]
    pass_on.wait()


def update(fragment, grad, weights, first, second, snapshot, momentum, total, back):
    full = jax.ShapeDtypeStruct(weights.shape, f32)
    part = jax.ShapeDtypeStruct(snapshot.shape, f32)
    vmem = pl.BlockSpec(memory_space=pltpu.VMEM)
    hbm = pl.BlockSpec(memory_space=pl.ANY)
    return pl.pallas_call(
        update_kernel,
        in_specs=[pl.BlockSpec(memory_space=pltpu.SMEM)] + [vmem] * 7 + [hbm],
        out_specs=[vmem] * 5 + [hbm],
        out_shape=[full] * 3 + [part] * 2 + [jax.ShapeDtypeStruct(back.shape, back.dtype)],
        scratch_shapes=[pltpu.VMEM(back.shape, back.dtype), pltpu.SemaphoreType.DMA((2,))],
        compiler_params=pltpu.CompilerParams(vmem_limit_bytes=60 * 2**20),
        name="update",
    )(fragment, grad, weights, first, second, snapshot, momentum, total, back)


def body(inputs, cotangent, params, first_moment, second_moment, snapshot, momentum, fragment):
    back, grad, total = projection(fragment, inputs[0], cotangent[0], params[0], snapshot)
    stepped, first, second, new_momentum, new_snapshot, input_grad = update(
        fragment, grad, params[0], first_moment[0], second_moment[0], snapshot, momentum, total, back
    )
    return (stepped[None], first[None], second[None], input_grad[None], new_momentum, new_snapshot)


def solution(mesh):
    return jax.shard_map(
        body,
        mesh=mesh,
        in_specs=(
            P("rep", "fsdp", None),
            P("rep", "fsdp", None),
            P("rep", "fsdp", None),
            P("rep", "fsdp", None),
            P("rep", "fsdp", None),
            P("fsdp", None),
            P("fsdp", None),
            P(),
        ),
        out_specs=(
            P("rep", "fsdp", None),
            P("rep", "fsdp", None),
            P("rep", "fsdp", None),
            P("rep", "fsdp", None),
            P("fsdp", None),
            P("fsdp", None),
        ),
        check_vma=False,
    )
```

```python
import functools

import jax
import jax.numpy as jnp
from jax import lax
from jax.experimental import pallas as pl
from jax.experimental.pallas import tpu as pltpu
from jax.sharding import PartitionSpec as P

beta_one = 0.9
beta_two = 0.95
inner_rate = 0.01
adam_eps = 1e-08
decay_rate = 0.1
outer_rate = 0.7
outer_mu = 0.9
mix_rate = 0.5

LANES = 128
CHUNK = 256
MESH = pl.DeviceIdType.MESH
f32 = jnp.float32
bf16 = jnp.bfloat16


def gelu_slope(t):
    c = 0.7978845608028654
    sq = t * t
    th = jnp.tanh(c * t * (1.0 + 0.044715 * sq))
    return 0.5 * (1.0 + th) + 0.5 * t * (1.0 - th * th) * (c * (1.0 + 3 * 0.044715 * sq))


def pair_kernel(
    frag_ref, x_hbm, cot_hbm, p_hbm, snap_hbm,
    out_ref, g_ref, total_ref,
    p_ref, snap_ref,
    xb, cb, w, g, rah, raf, rbh, rbf, pws, pwr, gps, gpr, bks, bkr, tmp, acc, pair_tmp, ds, dr, dq, dt, du,
    loc_sem, ag_send, ag_recv, rs_send, rs_recv, pw_send, pw_recv,
    x_send, x_recv, cot_send, cot_recv, bk_send, bk_recv, gp_send, gp_recv, d_send, d_recv,
):
    tok, width = x_hbm.shape
    rows, ffw = p_ref.shape
    half_cols = ffw // 2
    n_chunks = half_cols // CHUNK
    block = 2 * rows
    pad_rows = ds.shape[1]
    part_rows = dq.shape[0]
    core = lax.rem(lax.axis_index("rep"), 2)
    part = pl.ds(pl.multiple_of(core * (pad_rows - part_rows), 16), part_rows)
    frag = snap_ref.shape[1]
    cut = (block // 16 + 1) // 2 * 16
    n_x = x_send.shape[0]
    x_rows = tok // n_x
    n_bk = bk_send.shape[0]
    bk_rows = tok // (n_bk // 2)
    bk_cols = width // 2
    scale = width ** (-0.5)
    ahead = 6
    work_lag = 10
    done = work_lag + n_chunks

    f = lax.axis_index("fsdp")
    r = lax.axis_index("rep")
    yh = lax.rem(f, 2)
    x = lax.rem(lax.div(f, 2), 4)
    z = lax.div(f, 8)

    def device(zz, xx, yy):
        return {"fsdp": zz * 8 + xx * 2 + yy}

    peer = device(z, x, 1 - yh)
    sibling = {"rep": r + 1 - 2 * lax.rem(r, 2)}
    neighbour = {"rep": lax.rem(r + 2, 4)}
    place = {"x": x, "z": z}
    after = {a: lax.rem(place[a] + 1, 4) for a in place}
    before = {a: lax.rem(place[a] + 3, 4) for a in place}
    across = {a: lax.rem(place[a] + 2, 4) for a in place}
    right = {"x": device(z, after["x"], yh), "z": device(after["z"], x, yh)}
    left = {"x": device(z, before["x"], yh), "z": device(before["z"], x, yh)}
    first_axis = ("x", "z")
    second_axis = ("z", "x")
    my_base = yh * half_cols
    peer_base = (1 - yh) * half_cols

    def seg2(ref, u, p, i):
        return ref.at[u, i] if p == 0 else ref.at[u, :, i]

    def half2(ref, u, p, i, h):
        part = pl.ds(2 * h, 2)
        return ref.at[u, i, part] if p == 0 else ref.at[u, part, i]

    def seg1(ref, u, p, i):
        return ref.at[u, z, i] if p == 0 else ref.at[u, i, x]

    def half1(ref, u, p, i, h):
        part = pl.ds(0, cut) if h == 0 else pl.ds(cut, block - cut)
        return ref.at[u, z, i, part] if p == 0 else ref.at[u, i, x, part]

    def chunk_cols(c):
        return pl.ds(pl.multiple_of(c * CHUNK, CHUNK), CHUNK)

    def remote(src, dst, send, recv, to):
        return pltpu.make_async_remote_copy(
            src_ref=src, dst_ref=dst, send_sem=send, recv_sem=recv, device_id=to, device_id_type=MESH
        )

    def gather_copy(u, p, k):
        a, b = first_axis[p], second_axis[p]
        part = (
            lambda: seg1(w, u, p, place[a]),
            lambda: seg1(w, u, p, place[a]),
            lambda: half1(w, u, p, before[a], 0),
            lambda: half1(w, u, p, after[a], 1),
            lambda: seg2(w, u, p, place[b]),
            lambda: seg2(w, u, p, place[b]),
            lambda: half2(w, u, p, before[b], 0),
            lambda: half2(w, u, p, after[b], 1),
        )[k]()
        to = (right if k % 2 == 0 else left)[a if k < 4 else b]
        return remote(part, part, ag_send.at[u, k], ag_recv.at[u, k], to)

    def scatter_copy(u, p, k):
        a, b = first_axis[p], second_axis[p]
        src, dst = (
            lambda: (half2(g, u, p, across[b], 0), rah.at[u, 0]),
            lambda: (half2(g, u, p, across[b], 1), rah.at[u, 1]),
            lambda: (seg2(g, u, p, after[b]), raf.at[u, 0]),
            lambda: (seg2(g, u, p, before[b]), raf.at[u, 1]),
            lambda: (half1(g, u, p, across[a], 0), rbh.at[u, pl.ds(0, cut)]),
            lambda: (half1(g, u, p, across[a], 1), rbh.at[u, pl.ds(cut, block - cut)]),
            lambda: (seg1(g, u, p, after[a]), rbf.at[u, 0]),
            lambda: (seg1(g, u, p, before[a]), rbf.at[u, 1]),
        )[k]()
        to = (right if k % 2 == 0 else left)[b if k < 4 else a]
        return remote(src, dst, rs_send.at[u, k], rs_recv.at[u, k], to)

    def pw_copy(c):
        return remote(pws.at[c], pwr.at[c], pw_send.at[c], pw_recv.at[c], peer)

    def x_copy(i):
        return remote(
            x_hbm.at[pl.ds(i * x_rows, x_rows)], xb.at[pl.ds(tok + i * x_rows, x_rows)],
            x_send.at[i], x_recv.at[i], peer,
        )

    def cot_copy(c):
        cols = pl.ds(pl.multiple_of(peer_base + c * CHUNK, CHUNK), CHUNK)
        return remote(
            cot_hbm.at[:, cols], cb.at[pl.ds(tok, tok), chunk_cols(c)],
            cot_send.at[c], cot_recv.at[c], peer,
        )

    def bk_copy(i):
        return remote(bks.at[i], bkr.at[i], bk_send.at[i], bk_recv.at[i], peer)

    def gp_copy(c):
        return remote(gps.at[c], gpr.at[c], gp_send.at[c], gp_recv.at[c], peer)

    def d_copy(i):
        src, dst, to = (
            (ds.at[0], dr, sibling),
            (ds.at[1, part], dq, neighbour),
            (dt, du, sibling),
        )[i]
        return remote(src, dst, d_send.at[i], d_recv.at[i], to)

    def own_x():
        return pltpu.make_async_copy(x_hbm, xb.at[pl.ds(0, tok)], loc_sem.at[n_chunks])

    def own_params(h):
        cols = pl.ds(pl.multiple_of((my_base, peer_base)[h], LANES), half_cols)
        return pltpu.make_async_copy(p_hbm.at[:, cols], p_ref.at[:, cols], loc_sem.at[n_chunks + 2 + h])

    def own_snap():
        return pltpu.make_async_copy(snap_hbm, snap_ref, loc_sem.at[n_chunks + 1])

    def own_cot(c):
        cols = pl.ds(pl.multiple_of(my_base + c * CHUNK, CHUNK), CHUNK)
        return pltpu.make_async_copy(
            cot_hbm.at[:, cols], cb.at[pl.ds(0, tok), chunk_cols(c)], loc_sem.at[c]
        )

    def each(count, step):
        def run(i, carry):
            step(i)
            return carry
        lax.fori_loop(0, count, run, 0)

    def ranged(t, lag, step):
        @pl.when((t >= lag) & (t < lag + n_chunks))
        def _():
            step(t - lag)

    def both(step):
        def run(c):
            for p in range(2):
                step(2 * c + p, p)
        return run

    barrier = pltpu.get_barrier_semaphore()
    partners = (peer, right["x"], left["x"], right["z"], left["z"], sibling, neighbour)
    for partner in partners:
        pl.semaphore_signal(barrier, inc=1, device_id=partner, device_id_type=MESH)
    own_params(1).start()
    own_params(0).start()
    own_snap().start()
    own_params(1).wait()
    pl.semaphore_wait(barrier, len(partners))

    def prepare(c):
        parts = []
        for h in range(2):
            cols = pl.ds(pl.multiple_of(peer_base + c * CHUNK + h * LANES, LANES), LANES)
            parts.append(p_ref[:, cols])
        pws[c] = jnp.concatenate(parts, axis=0).astype(bf16)
        pw_copy(c).start()

    each(n_chunks, prepare)
    each(n_x, lambda i: x_copy(i).start())
    own_x().start()
    each(n_chunks, lambda c: own_cot(c).start())
    own_snap().wait()
    own_params(0).wait()
    local = p_ref[:, :frag]
    for i in range(1, ffw // frag):
        local = jnp.where(frag_ref[0] == i, p_ref[:, i * frag : (i + 1) * frag], local)
    delta = snap_ref[...] - local
    ds[0] = jnp.concatenate([delta, jnp.zeros((pad_rows - rows, frag), f32)], axis=0).astype(bf16)

    d_copy(0).start()

    def chunk_weights(c):
        return jnp.concatenate(
            [w[2 * c].reshape(width, LANES), w[2 * c + 1].reshape(width, LANES)], axis=1
        )

    def hidden(c, start):
        at = pl.ds(start, tok)
        pre = jnp.dot(xb[at, :], chunk_weights(c), preferred_element_type=f32) * scale
        cot = cb[at, chunk_cols(c)].astype(f32)
        cb[at, chunk_cols(c)] = (gelu_slope(pre) * cot * scale).astype(bf16)

    def gather_own(c):
        pw_copy(c).wait_recv()
        pair_tmp[...] = pwr[c].astype(f32)
        for h in range(2):
            cols = pl.ds(pl.multiple_of(my_base + c * CHUNK + h * LANES, LANES), LANES)
            tmp[pl.ds(pl.multiple_of(yh * rows, 8), rows), :] = p_ref[:, cols]
            tmp[pl.ds(pl.multiple_of((1 - yh) * rows, 8), rows), :] = pair_tmp[pl.ds(h * rows, rows), :]
            w[2 * c + h, z, x] = tmp[...].astype(bf16)
            gather_copy(2 * c + h, h, 0).start()
            gather_copy(2 * c + h, h, 1).start()

    def gather_forward(k):
        def step(u, p):
            gather_copy(u, p, k).wait_recv()
            gather_copy(u, p, k + 2).start()
            gather_copy(u, p, k + 1).wait_recv()
            gather_copy(u, p, k + 3).start()
        return both(step)

    @both
    def gather_second(u, p):
        gather_copy(u, p, 2).wait_recv()
        gather_copy(u, p, 3).wait_recv()
        gather_copy(u, p, 4).start()
        gather_copy(u, p, 5).start()

    @both
    def gather_end(u, p):
        gather_copy(u, p, 6).wait_recv()
        gather_copy(u, p, 7).wait_recv()

    def own_hidden(c):
        gather_end(c)
        own_cot(c).wait()
        hidden(c, 0)

    def add_into(ref, other):
        ref[...] = (ref[...].astype(f32) + other[...].astype(f32)).astype(bf16)

    def back_part(n, start, units):
        part = jnp.concatenate(
            [w[u, pl.ds(2 * n, 2)].reshape(bk_cols, LANES) for u in units], axis=1
        )
        cols = slice(units[0] * LANES, (units[-1] + 1) * LANES)
        return lax.dot_general(
            cb[pl.ds(start, tok), cols], part, (((1,), (1,)), ((), ())), preferred_element_type=f32
        )

    def send_back(n, term):
        for m in range(n_bk // 2):
            i = n * (n_bk // 2) + m
            bks[i] = term[m * bk_rows : (m + 1) * bk_rows].astype(bf16)
            bk_copy(i).start()

    middle = n_chunks // 2
    early = range(2 * middle)
    late = range(2 * middle, 2 * n_chunks - 2)
    final = range(2 * n_chunks - 2, 2 * n_chunks)

    def work(c):
        @pl.when(c == middle)
        def _():
            acc[0] = back_part(0, tok, early)

        @pl.when(c == n_chunks - 1)
        def _():
            d_copy(1).start()
            acc[0] = acc[0] + back_part(0, tok, late)

        cot_copy(c).wait_recv()

        @pl.when(c + ahead < n_chunks)
        def _():
            cot_copy(c + ahead).start()

        hidden(c, tok)

        @pl.when(c == n_chunks - 1)
        def _():
            send_back(0, acc[0] + back_part(0, tok, final))

        term = lax.dot_general(
            xb[...], cb[:, chunk_cols(c)], (((0,), (0,)), ((), ())), preferred_element_type=f32
        ).astype(bf16)
        for h in range(2):
            g[2 * c + h] = term[:, h * LANES : (h + 1) * LANES].reshape(4, 4, block, LANES)
        for p in range(2):
            scatter_copy(2 * c + p, p, 0).start()
            scatter_copy(2 * c + p, p, 1).start()

    @both
    def scatter_second(u, p):
        b = second_axis[p]
        scatter_copy(u, p, 0).wait_recv()
        add_into(half2(g, u, p, after[b], 0), rah.at[u, 0])
        scatter_copy(u, p, 2).start()
        scatter_copy(u, p, 1).wait_recv()
        add_into(half2(g, u, p, before[b], 1), rah.at[u, 1])
        scatter_copy(u, p, 3).start()

    @both
    def scatter_third(u, p):
        b = second_axis[p]
        scatter_copy(u, p, 2).wait_recv()
        scatter_copy(u, p, 3).wait_recv()
        mine = seg2(g, u, p, place[b])
        mine[...] = (
            mine[...].astype(f32) + raf[u, 0].astype(f32) + raf[u, 1].astype(f32)
        ).astype(bf16)
        scatter_copy(u, p, 4).start()
        scatter_copy(u, p, 5).start()

    @both
    def scatter_fourth(u, p):
        a = first_axis[p]
        scatter_copy(u, p, 4).wait_recv()
        add_into(half1(g, u, p, after[a], 0), rbh.at[u, pl.ds(0, cut)])
        scatter_copy(u, p, 6).start()
        scatter_copy(u, p, 5).wait_recv()
        add_into(half1(g, u, p, before[a], 1), rbh.at[u, pl.ds(cut, block - cut)])
        scatter_copy(u, p, 7).start()

    @both
    def scatter_end(u, p):
        a = first_axis[p]
        for k in range(6):
            scatter_copy(u, p, k).wait_send()
        scatter_copy(u, p, 6).wait_recv()
        scatter_copy(u, p, 7).wait_recv()
        mine = seg1(g, u, p, place[a])
        tmp[...] = mine[...].astype(f32) + rbf[u, 0].astype(f32) + rbf[u, 1].astype(f32)
        pair_tmp[pl.ds(p * rows, rows), :] = tmp[pl.ds(pl.multiple_of((1 - yh) * rows, 8), rows), :]
        cols = pl.ds(pl.multiple_of(my_base + u * LANES, LANES), LANES)
        g_ref[:, cols] = tmp[pl.ds(pl.multiple_of(yh * rows, 8), rows), :]
        if p == 1:
            c = lax.div(u, 2)
            gps[c] = pair_tmp[...].astype(bf16)
            gp_copy(c).start()

    def keep_back(n):
        acc[n] = back_part(n, 0, range(2 * n_chunks))

    def settle(c):
        pw_copy(c).wait_send()
        cot_copy(c).wait_send()
        for p in range(2):
            for k in range(8):
                gather_copy(2 * c + p, p, k).wait_send()

    def tick(t):
        ranged(t, 0, gather_own)
        ranged(t, 1, gather_forward(0))
        ranged(t, 2, gather_second)
        ranged(t, 3, gather_forward(4))

        @pl.when(t == 4)
        def _():
            own_x().wait()

        ranged(t, 4, own_hidden)

        @pl.when(t == 1)
        def _():
            d_copy(0).wait_recv()
            ds[1] = (ds[0].astype(f32) + dr[...].astype(f32)).astype(bf16)

        @pl.when(t == 8)
        def _():
            for c in range(ahead):
                cot_copy(c).start()

        @pl.when(t == work_lag)
        def _():
            for i in range(n_x):
                x_copy(i).wait_recv()

        ranged(t, work_lag, work)

        @pl.when(t == done)
        def _():
            send_back(1, back_part(1, tok, range(2 * n_chunks)))

        @pl.when((t >= done + 1) & (t < done + 3))
        def _():
            keep_back(t - done - 1)

        ranged(t, work_lag + 2, settle)
        ranged(t, work_lag + 3, scatter_second)
        ranged(t, work_lag + 6, scatter_third)
        ranged(t, work_lag + 8, scatter_fourth)
        ranged(t, work_lag + 9, scatter_end)

    each(n_chunks + work_lag + 9, tick)

    def finish_back(i):
        bk_copy(i).wait_recv()
        n, m = lax.div(i, n_bk // 2), lax.rem(i, n_bk // 2)
        at = pl.ds(pl.multiple_of(m * bk_rows, 16), bk_rows)
        cols = pl.ds(pl.multiple_of(n * bk_cols, LANES), bk_cols)
        out_ref[at, cols] = (acc[n, at, :] + bkr[i].astype(f32)).astype(bf16)


    def finish_grad(c):
        gp_copy(c).wait_recv()
        pair_tmp[...] = gpr[c].astype(f32)
        for h in range(2):
            cols = pl.ds(pl.multiple_of(peer_base + c * CHUNK + h * LANES, LANES), LANES)
            g_ref[:, cols] = pair_tmp[pl.ds(h * rows, rows), :]

    d_copy(1).wait_recv()
    dt[...] = ds[1, part].astype(f32) + dq[...].astype(f32)
    d_copy(2).start()
    each(n_bk, finish_back)
    d_copy(2).wait_recv()
    total_ref[...] = jnp.where(
        core == 0,
        jnp.concatenate([dt[...], du[2 * part_rows - pad_rows :]], axis=0)[:rows],
        jnp.concatenate([du[...], dt[2 * part_rows - pad_rows :]], axis=0)[:rows],
    )
    each(n_chunks, finish_grad)

    def finish(c):
        gp_copy(c).wait_send()
        for p in range(2):
            for k in range(6, 8):
                scatter_copy(2 * c + p, p, k).wait_send()

    each(n_chunks, finish)
    each(n_x, lambda i: x_copy(i).wait_send())
    for i in range(3):
        d_copy(i).wait_send()

    def finish_out(i):
        bk_copy(i).wait_send()

    each(n_bk, finish_out)


def projection(fragment, acts, cot, weights, snapshot):
    tok, width = acts.shape
    rows, ffw = weights.shape
    frag = snapshot.shape[1]
    units = ffw // 2 // LANES
    chunks = units // 2
    block = 2 * rows
    pad_rows = (rows + 15) // 16 * 16
    part_rows = (pad_rows // 16 + 1) // 2 * 16
    n_x, n_bk = 3, 6
    dma = pltpu.SemaphoreType.DMA
    vmem = pltpu.VMEM
    return pl.pallas_call(
        pair_kernel,
        out_shape=(
            vmem((tok, width), bf16),
            vmem((rows, ffw), f32),
            vmem((rows, frag), f32),
        ),
        in_specs=[
            pl.BlockSpec(memory_space=pltpu.SMEM),
            pl.BlockSpec(memory_space=pl.ANY),
            pl.BlockSpec(memory_space=pl.ANY),
            pl.BlockSpec(memory_space=pl.ANY),
            pl.BlockSpec(memory_space=pl.ANY),
        ],
        out_specs=(pl.BlockSpec(memory_space=vmem),) * 3,
        scratch_shapes=[
            vmem((rows, ffw), f32),
            vmem((rows, frag), f32),
            vmem((2 * tok, width), bf16),
            vmem((2 * tok, ffw // 2), bf16),
            vmem((units, 4, 4, block, LANES), bf16),
            vmem((units, 4, 4, block, LANES), bf16),
            vmem((units, 2, 2, block, LANES), bf16),
            vmem((units, 2, 4, block, LANES), bf16),
            vmem((units, block, LANES), bf16),
            vmem((units, 2, block, LANES), bf16),
            vmem((chunks, block, LANES), bf16),
            vmem((chunks, block, LANES), bf16),
            vmem((chunks, block, LANES), bf16),
            vmem((chunks, block, LANES), bf16),
            vmem((n_bk, tok // (n_bk // 2), width // 2), bf16),
            vmem((n_bk, tok // (n_bk // 2), width // 2), bf16),
            vmem((block, LANES), f32),
            vmem((2, tok, width // 2), f32),
            vmem((block, LANES), f32),
            vmem((2, pad_rows, frag), bf16),
            vmem((pad_rows, frag), bf16),
            vmem((part_rows, frag), bf16),
            vmem((part_rows, frag), f32),
            vmem((part_rows, frag), f32),
            dma((chunks + 4,)),
            dma((units, 8)), dma((units, 8)),
            dma((units, 8)), dma((units, 8)),
            dma((chunks,)), dma((chunks,)),
            dma((n_x,)), dma((n_x,)),
            dma((chunks,)), dma((chunks,)),
            dma((n_bk,)), dma((n_bk,)),
            dma((chunks,)), dma((chunks,)),
            dma((3,)), dma((3,)),
        ],
        compiler_params=pltpu.CompilerParams(
            collective_id=1, has_side_effects=True, vmem_limit_bytes=53 * 2**20
        ),
        cost_estimate=pl.CostEstimate(
            flops=6 * tok * width * ffw, bytes_accessed=16 * tok * width, transcendentals=tok * ffw
        ),
        name="pair_projection",
    )(fragment, acts, cot, weights, snapshot)


def update_kernel(
    frag_ref, g_ref, p_ref, m_ref, v_ref, snap_ref, mom_ref, total_ref, back_ref,
    p_out, m_out, v_out, mom_out, snap_out, back_out,
    new_p, new_m, new_v, new_mom, new_snap, wide_sem, sem,
):
    frag = snap_ref.shape[1]
    blocks = wide_sem.shape[0]
    step = p_ref.shape[0] // blocks
    pass_on = pltpu.make_async_copy(back_ref, back_out, sem.at[0])
    pass_on.start()
    outer = total_ref[...] * 0.25
    mom = outer_mu * mom_ref[...] + outer
    new_mom[...] = mom
    new_snap[...] = snap_ref[...] - outer_rate * (outer + outer_mu * mom)
    copies = [
        pass_on,
        pltpu.make_async_copy(new_mom, mom_out, sem.at[1]),
        pltpu.make_async_copy(new_snap, snap_out, sem.at[2]),
    ]
    copies[1].start()
    copies[2].start()
    cols = pl.ds(pl.multiple_of(frag_ref[0] * frag, LANES), frag)
    for b in range(blocks):
        at = pl.ds(b * step, step)
        grad = g_ref[at, :]
        weights = p_ref[at, :]
        first = beta_one * m_ref[at, :] + (1.0 - beta_one) * grad
        second = beta_two * v_ref[at, :] + (1.0 - beta_two) * grad * grad
        new_m[at, :] = first
        new_v[at, :] = second
        new_p[at, :] = weights - inner_rate * (
            first / (jnp.sqrt(second) + adam_eps) + decay_rate * weights
        )
        new_p[at, cols] = mix_rate * new_snap[at, :] + (1.0 - mix_rate) * new_p[at, cols]
        for i, (src, dst) in enumerate(((new_p, p_out), (new_m, m_out), (new_v, v_out))):
            copy = pltpu.make_async_copy(src.at[at], dst.at[at], wide_sem.at[b, i])
            copy.start()
            copies.append(copy)
    for copy in copies:
        copy.wait()


def update(fragment, grad, weights, first, second, snapshot, momentum, total, back):
    full = jax.ShapeDtypeStruct(weights.shape, f32)
    part = jax.ShapeDtypeStruct(snapshot.shape, f32)
    vmem = pl.BlockSpec(memory_space=pltpu.VMEM)
    hbm = pl.BlockSpec(memory_space=pl.ANY)
    return pl.pallas_call(
        update_kernel,
        in_specs=[pl.BlockSpec(memory_space=pltpu.SMEM)] + [vmem] * 8,
        out_specs=[hbm] * 6,
        out_shape=[full] * 3 + [part] * 2 + [jax.ShapeDtypeStruct(back.shape, back.dtype)],
        scratch_shapes=[pltpu.VMEM(weights.shape, f32)] * 3
        + [pltpu.VMEM(snapshot.shape, f32)] * 2
        + [pltpu.SemaphoreType.DMA((3, 3)), pltpu.SemaphoreType.DMA((3,))],
        compiler_params=pltpu.CompilerParams(vmem_limit_bytes=24 * 2**20),
        name="update",
    )(fragment, grad, weights, first, second, snapshot, momentum, total, back)


def body(inputs, cotangent, params, first_moment, second_moment, snapshot, momentum, fragment):
    back, grad, total = projection(fragment, inputs[0], cotangent[0], params[0], snapshot)
    stepped, first, second, new_momentum, new_snapshot, input_grad = update(
        fragment, grad, params[0], first_moment[0], second_moment[0], snapshot, momentum, total, back
    )
    return (stepped[None], first[None], second[None], input_grad[None], new_momentum, new_snapshot)


def solution(mesh):
    return jax.shard_map(
        body,
        mesh=mesh,
        in_specs=(
            P("rep", "fsdp", None),
            P("rep", "fsdp", None),
            P("rep", "fsdp", None),
            P("rep", "fsdp", None),
            P("rep", "fsdp", None),
            P("fsdp", None),
            P("fsdp", None),
            P(),
        ),
        out_specs=(
            P("rep", "fsdp", None),
            P("rep", "fsdp", None),
            P("rep", "fsdp", None),
            P("rep", "fsdp", None),
            P("fsdp", None),
            P("fsdp", None),
        ),
        check_vma=False,
    )
```

```python
import functools

import jax
import jax.numpy as jnp
from jax import lax
from jax.experimental import pallas as pl
from jax.experimental.pallas import tpu as pltpu
from jax.sharding import PartitionSpec as P

beta_one = 0.9
beta_two = 0.95
inner_rate = 0.01
adam_eps = 1e-08
decay_rate = 0.1
outer_rate = 0.7
outer_mu = 0.9
mix_rate = 0.5

LANES = 128
CHUNK = 256
MESH = pl.DeviceIdType.MESH
f32 = jnp.float32
bf16 = jnp.bfloat16


def gelu_slope(t):
    c = 0.7978845608028654
    sq = t * t
    th = jnp.tanh(c * t * (1.0 + 0.044715 * sq))
    return 0.5 * (1.0 + th) + 0.5 * t * (1.0 - th * th) * (c * (1.0 + 3 * 0.044715 * sq))


def pair_kernel(
    frag_ref, x_hbm, cot_hbm, p_hbm, snap_hbm,
    out_ref, g_ref, total_ref,
    p_ref, snap_ref,
    xb, cb, w, g, rah, raf, rbh, rbf, pws, pwr, gps, gpr, bks, bkr, tmp, acc, pair_tmp, ds, dr, dq, dt, du,
    loc_sem, ag_send, ag_recv, rs_send, rs_recv, pw_send, pw_recv,
    x_send, x_recv, cot_send, cot_recv, bk_send, bk_recv, gp_send, gp_recv, d_send, d_recv,
):
    tok, width = x_hbm.shape
    rows, ffw = p_ref.shape
    half_cols = ffw // 2
    n_chunks = half_cols // CHUNK
    block = 2 * rows
    pad_rows = ds.shape[1]
    part_rows = dq.shape[0]
    core = lax.rem(lax.axis_index("rep"), 2)
    parts = (pl.ds(0, part_rows), pl.ds(part_rows, pad_rows - part_rows))
    frag = snap_ref.shape[1]
    cut = (block // 16 + 1) // 2 * 16
    n_x = x_send.shape[0]
    x_rows = tok // n_x
    n_bk = bk_send.shape[0]
    bk_rows = tok // (n_bk // 2)
    bk_cols = width // 2
    scale = width ** (-0.5)
    ahead = 6
    work_lag = 10
    done = work_lag + n_chunks

    f = lax.axis_index("fsdp")
    r = lax.axis_index("rep")
    yh = lax.rem(f, 2)
    x = lax.rem(lax.div(f, 2), 4)
    z = lax.div(f, 8)

    def device(zz, xx, yy):
        return {"fsdp": zz * 8 + xx * 2 + yy}

    peer = device(z, x, 1 - yh)
    sibling = {"rep": r + 1 - 2 * lax.rem(r, 2)}
    neighbour = {"rep": lax.rem(r + 2, 4)}
    place = {"x": x, "z": z}
    after = {a: lax.rem(place[a] + 1, 4) for a in place}
    before = {a: lax.rem(place[a] + 3, 4) for a in place}
    across = {a: lax.rem(place[a] + 2, 4) for a in place}
    right = {"x": device(z, after["x"], yh), "z": device(after["z"], x, yh)}
    left = {"x": device(z, before["x"], yh), "z": device(before["z"], x, yh)}
    first_axis = ("x", "z")
    second_axis = ("z", "x")
    my_base = yh * half_cols
    peer_base = (1 - yh) * half_cols

    def seg2(ref, u, p, i):
        return ref.at[u, i] if p == 0 else ref.at[u, :, i]

    def half2(ref, u, p, i, h):
        part = pl.ds(2 * h, 2)
        return ref.at[u, i, part] if p == 0 else ref.at[u, part, i]

    def seg1(ref, u, p, i):
        return ref.at[u, z, i] if p == 0 else ref.at[u, i, x]

    def half1(ref, u, p, i, h):
        part = pl.ds(0, cut) if h == 0 else pl.ds(cut, block - cut)
        return ref.at[u, z, i, part] if p == 0 else ref.at[u, i, x, part]

    def chunk_cols(c):
        return pl.ds(pl.multiple_of(c * CHUNK, CHUNK), CHUNK)

    def remote(src, dst, send, recv, to):
        return pltpu.make_async_remote_copy(
            src_ref=src, dst_ref=dst, send_sem=send, recv_sem=recv, device_id=to, device_id_type=MESH
        )

    def gather_copy(u, p, k):
        a, b = first_axis[p], second_axis[p]
        part = (
            lambda: seg1(w, u, p, place[a]),
            lambda: seg1(w, u, p, place[a]),
            lambda: half1(w, u, p, before[a], 0),
            lambda: half1(w, u, p, after[a], 1),
            lambda: seg2(w, u, p, place[b]),
            lambda: seg2(w, u, p, place[b]),
            lambda: half2(w, u, p, before[b], 0),
            lambda: half2(w, u, p, after[b], 1),
        )[k]()
        to = (right if k % 2 == 0 else left)[a if k < 4 else b]
        return remote(part, part, ag_send.at[u, k], ag_recv.at[u, k], to)

    def scatter_copy(u, p, k):
        a, b = first_axis[p], second_axis[p]
        src, dst = (
            lambda: (half2(g, u, p, across[b], 0), rah.at[u, 0]),
            lambda: (half2(g, u, p, across[b], 1), rah.at[u, 1]),
            lambda: (seg2(g, u, p, after[b]), raf.at[u, 0]),
            lambda: (seg2(g, u, p, before[b]), raf.at[u, 1]),
            lambda: (half1(g, u, p, across[a], 0), rbh.at[u, pl.ds(0, cut)]),
            lambda: (half1(g, u, p, across[a], 1), rbh.at[u, pl.ds(cut, block - cut)]),
            lambda: (seg1(g, u, p, after[a]), rbf.at[u, 0]),
            lambda: (seg1(g, u, p, before[a]), rbf.at[u, 1]),
        )[k]()
        to = (right if k % 2 == 0 else left)[b if k < 4 else a]
        return remote(src, dst, rs_send.at[u, k], rs_recv.at[u, k], to)

    def pw_copy(c):
        return remote(pws.at[c], pwr.at[c], pw_send.at[c], pw_recv.at[c], peer)

    def x_copy(i):
        return remote(
            x_hbm.at[pl.ds(i * x_rows, x_rows)], xb.at[pl.ds(tok + i * x_rows, x_rows)],
            x_send.at[i], x_recv.at[i], peer,
        )

    def cot_copy(c):
        cols = pl.ds(pl.multiple_of(peer_base + c * CHUNK, CHUNK), CHUNK)
        return remote(
            cot_hbm.at[:, cols], cb.at[pl.ds(tok, tok), chunk_cols(c)],
            cot_send.at[c], cot_recv.at[c], peer,
        )

    def bk_copy(i):
        return remote(bks.at[i], bkr.at[i], bk_send.at[i], bk_recv.at[i], peer)

    def gp_copy(c):
        return remote(gps.at[c], gpr.at[c], gp_send.at[c], gp_recv.at[c], peer)

    def d_copy(i):
        src, dst, to = (
            (ds.at[0], dr, sibling),
            (dt, du, sibling),
        )[i]
        return remote(src, dst, d_send.at[i], d_recv.at[i], to)

    def on_core(step):
        for which, part in enumerate(parts):
            count = part.size
            copy = remote(
                ds.at[1, part], dq.at[pl.ds(0, count)], d_send.at[2], d_recv.at[2], neighbour
            )
            pl.when(core == which)(functools.partial(step, copy, part, count))

    def add_half(copy, part, count):
        copy.wait_recv()
        dt[:count] = ds[1, part].astype(f32) + dq[:count].astype(f32)

    def own_x():
        return pltpu.make_async_copy(x_hbm, xb.at[pl.ds(0, tok)], loc_sem.at[n_chunks])

    def own_params(h):
        cols = pl.ds(pl.multiple_of((my_base, peer_base)[h], LANES), half_cols)
        return pltpu.make_async_copy(p_hbm.at[:, cols], p_ref.at[:, cols], loc_sem.at[n_chunks + 2 + h])

    def own_snap():
        return pltpu.make_async_copy(snap_hbm, snap_ref, loc_sem.at[n_chunks + 1])

    def own_cot(c):
        cols = pl.ds(pl.multiple_of(my_base + c * CHUNK, CHUNK), CHUNK)
        return pltpu.make_async_copy(
            cot_hbm.at[:, cols], cb.at[pl.ds(0, tok), chunk_cols(c)], loc_sem.at[c]
        )

    def each(count, step):
        def run(i, carry):
            step(i)
            return carry
        lax.fori_loop(0, count, run, 0)

    def ranged(t, lag, step):
        @pl.when((t >= lag) & (t < lag + n_chunks))
        def _():
            step(t - lag)

    def both(step):
        def run(c):
            for p in range(2):
                step(2 * c + p, p)
        return run

    barrier = pltpu.get_barrier_semaphore()
    partners = (peer, right["x"], left["x"], right["z"], left["z"], sibling, neighbour)
    for partner in partners:
        pl.semaphore_signal(barrier, inc=1, device_id=partner, device_id_type=MESH)
    own_params(1).start()
    own_params(0).start()
    own_snap().start()
    own_params(1).wait()
    pl.semaphore_wait(barrier, len(partners))

    def prepare(c):
        parts = []
        for h in range(2):
            cols = pl.ds(pl.multiple_of(peer_base + c * CHUNK + h * LANES, LANES), LANES)
            parts.append(p_ref[:, cols])
        pws[c] = jnp.concatenate(parts, axis=0).astype(bf16)
        pw_copy(c).start()

    each(n_chunks, prepare)
    each(n_x, lambda i: x_copy(i).start())
    own_x().start()
    each(n_chunks, lambda c: own_cot(c).start())
    own_snap().wait()
    own_params(0).wait()
    local = p_ref[:, :frag]
    for i in range(1, ffw // frag):
        local = jnp.where(frag_ref[0] == i, p_ref[:, i * frag : (i + 1) * frag], local)
    delta = snap_ref[...] - local
    ds[0] = jnp.concatenate([delta, jnp.zeros((pad_rows - rows, frag), f32)], axis=0).astype(bf16)

    d_copy(0).start()

    def chunk_weights(c):
        return jnp.concatenate(
            [w[2 * c].reshape(width, LANES), w[2 * c + 1].reshape(width, LANES)], axis=1
        )

    def hidden(c, start):
        at = pl.ds(start, tok)
        pre = jnp.dot(xb[at, :], chunk_weights(c), preferred_element_type=f32) * scale
        cot = cb[at, chunk_cols(c)].astype(f32)
        cb[at, chunk_cols(c)] = (gelu_slope(pre) * cot * scale).astype(bf16)

    def gather_own(c):
        pw_copy(c).wait_recv()
        pair_tmp[...] = pwr[c].astype(f32)
        for h in range(2):
            cols = pl.ds(pl.multiple_of(my_base + c * CHUNK + h * LANES, LANES), LANES)
            tmp[pl.ds(pl.multiple_of(yh * rows, 8), rows), :] = p_ref[:, cols]
            tmp[pl.ds(pl.multiple_of((1 - yh) * rows, 8), rows), :] = pair_tmp[pl.ds(h * rows, rows), :]
            w[2 * c + h, z, x] = tmp[...].astype(bf16)
            gather_copy(2 * c + h, h, 0).start()
            gather_copy(2 * c + h, h, 1).start()

    def gather_forward(k):
        def step(u, p):
            gather_copy(u, p, k).wait_recv()
            gather_copy(u, p, k + 2).start()
            gather_copy(u, p, k + 1).wait_recv()
            gather_copy(u, p, k + 3).start()
        return both(step)

    @both
    def gather_second(u, p):
        gather_copy(u, p, 2).wait_recv()
        gather_copy(u, p, 3).wait_recv()
        gather_copy(u, p, 4).start()
        gather_copy(u, p, 5).start()

    @both
    def gather_end(u, p):
        gather_copy(u, p, 6).wait_recv()
        gather_copy(u, p, 7).wait_recv()

    def own_hidden(c):
        gather_end(c)
        own_cot(c).wait()
        hidden(c, 0)

    def add_into(ref, other):
        ref[...] = (ref[...].astype(f32) + other[...].astype(f32)).astype(bf16)

    def back_part(n, start, units):
        part = jnp.concatenate(
            [w[u, pl.ds(2 * n, 2)].reshape(bk_cols, LANES) for u in units], axis=1
        )
        cols = slice(units[0] * LANES, (units[-1] + 1) * LANES)
        return lax.dot_general(
            cb[pl.ds(start, tok), cols], part, (((1,), (1,)), ((), ())), preferred_element_type=f32
        )

    def send_back(n, term):
        for m in range(n_bk // 2):
            i = n * (n_bk // 2) + m
            bks[i] = term[m * bk_rows : (m + 1) * bk_rows].astype(bf16)
            bk_copy(i).start()

    middle = n_chunks // 2
    early = range(2 * middle)
    late = range(2 * middle, 2 * n_chunks - 2)
    final = range(2 * n_chunks - 2, 2 * n_chunks)

    def work(c):
        @pl.when(c == middle)
        def _():
            acc[0] = back_part(0, tok, early)

        @pl.when(c == n_chunks - 1)
        def _():
            on_core(lambda copy, part, count: copy.start())
            acc[0] = acc[0] + back_part(0, tok, late)

        cot_copy(c).wait_recv()

        @pl.when(c + ahead < n_chunks)
        def _():
            cot_copy(c + ahead).start()

        hidden(c, tok)

        @pl.when(c == n_chunks - 1)
        def _():
            send_back(0, acc[0] + back_part(0, tok, final))

        term = lax.dot_general(
            xb[...], cb[:, chunk_cols(c)], (((0,), (0,)), ((), ())), preferred_element_type=f32
        ).astype(bf16)
        for h in range(2):
            g[2 * c + h] = term[:, h * LANES : (h + 1) * LANES].reshape(4, 4, block, LANES)
        for p in range(2):
            scatter_copy(2 * c + p, p, 0).start()
            scatter_copy(2 * c + p, p, 1).start()

    @both
    def scatter_second(u, p):
        b = second_axis[p]
        scatter_copy(u, p, 0).wait_recv()
        add_into(half2(g, u, p, after[b], 0), rah.at[u, 0])
        scatter_copy(u, p, 2).start()
        scatter_copy(u, p, 1).wait_recv()
        add_into(half2(g, u, p, before[b], 1), rah.at[u, 1])
        scatter_copy(u, p, 3).start()

    @both
    def scatter_third(u, p):
        b = second_axis[p]
        scatter_copy(u, p, 2).wait_recv()
        scatter_copy(u, p, 3).wait_recv()
        mine = seg2(g, u, p, place[b])
        mine[...] = (
            mine[...].astype(f32) + raf[u, 0].astype(f32) + raf[u, 1].astype(f32)
        ).astype(bf16)
        scatter_copy(u, p, 4).start()
        scatter_copy(u, p, 5).start()

    @both
    def scatter_fourth(u, p):
        a = first_axis[p]
        scatter_copy(u, p, 4).wait_recv()
        add_into(half1(g, u, p, after[a], 0), rbh.at[u, pl.ds(0, cut)])
        scatter_copy(u, p, 6).start()
        scatter_copy(u, p, 5).wait_recv()
        add_into(half1(g, u, p, before[a], 1), rbh.at[u, pl.ds(cut, block - cut)])
        scatter_copy(u, p, 7).start()

    @both
    def scatter_end(u, p):
        a = first_axis[p]
        for k in range(6):
            scatter_copy(u, p, k).wait_send()
        scatter_copy(u, p, 6).wait_recv()
        scatter_copy(u, p, 7).wait_recv()
        mine = seg1(g, u, p, place[a])
        tmp[...] = mine[...].astype(f32) + rbf[u, 0].astype(f32) + rbf[u, 1].astype(f32)
        pair_tmp[pl.ds(p * rows, rows), :] = tmp[pl.ds(pl.multiple_of((1 - yh) * rows, 8), rows), :]
        cols = pl.ds(pl.multiple_of(my_base + u * LANES, LANES), LANES)
        g_ref[:, cols] = tmp[pl.ds(pl.multiple_of(yh * rows, 8), rows), :]
        if p == 1:
            c = lax.div(u, 2)
            gps[c] = pair_tmp[...].astype(bf16)
            gp_copy(c).start()

    def keep_back(n):
        acc[n] = back_part(n, 0, range(2 * n_chunks))

    def settle(c):
        pw_copy(c).wait_send()
        cot_copy(c).wait_send()
        for p in range(2):
            for k in range(8):
                gather_copy(2 * c + p, p, k).wait_send()

    def tick(t):
        ranged(t, 0, gather_own)
        ranged(t, 1, gather_forward(0))
        ranged(t, 2, gather_second)
        ranged(t, 3, gather_forward(4))

        @pl.when(t == 4)
        def _():
            own_x().wait()

        ranged(t, 4, own_hidden)

        @pl.when(t == 1)
        def _():
            d_copy(0).wait_recv()
            ds[1] = (ds[0].astype(f32) + dr[...].astype(f32)).astype(bf16)

        @pl.when(t == 8)
        def _():
            for c in range(ahead):
                cot_copy(c).start()

        @pl.when(t == work_lag)
        def _():
            for i in range(n_x):
                x_copy(i).wait_recv()

        ranged(t, work_lag, work)

        @pl.when(t == done)
        def _():
            send_back(1, back_part(1, tok, range(2 * n_chunks)))

        @pl.when((t >= done + 1) & (t < done + 3))
        def _():
            keep_back(t - done - 1)

        ranged(t, work_lag + 2, settle)
        ranged(t, work_lag + 3, scatter_second)
        ranged(t, work_lag + 6, scatter_third)
        ranged(t, work_lag + 8, scatter_fourth)
        ranged(t, work_lag + 9, scatter_end)

    each(n_chunks + work_lag + 9, tick)

    def finish_back(i):
        bk_copy(i).wait_recv()
        n, m = lax.div(i, n_bk // 2), lax.rem(i, n_bk // 2)
        at = pl.ds(pl.multiple_of(m * bk_rows, 16), bk_rows)
        cols = pl.ds(pl.multiple_of(n * bk_cols, LANES), bk_cols)
        out_ref[at, cols] = (acc[n, at, :] + bkr[i].astype(f32)).astype(bf16)


    def finish_grad(c):
        gp_copy(c).wait_recv()
        pair_tmp[...] = gpr[c].astype(f32)
        for h in range(2):
            cols = pl.ds(pl.multiple_of(peer_base + c * CHUNK + h * LANES, LANES), LANES)
            g_ref[:, cols] = pair_tmp[pl.ds(h * rows, rows), :]

    on_core(add_half)
    d_copy(1).start()
    each(n_bk, finish_back)
    d_copy(1).wait_recv()
    total_ref[...] = jnp.where(
        core == 0,
        jnp.concatenate([dt[...], du[: pad_rows - part_rows]], axis=0)[:rows],
        jnp.concatenate([du[...], dt[: pad_rows - part_rows]], axis=0)[:rows],
    )
    each(n_chunks, finish_grad)

    def finish(c):
        gp_copy(c).wait_send()
        for p in range(2):
            for k in range(6, 8):
                scatter_copy(2 * c + p, p, k).wait_send()

    each(n_chunks, finish)
    each(n_x, lambda i: x_copy(i).wait_send())
    for i in range(2):
        d_copy(i).wait_send()
    on_core(lambda copy, part, count: copy.wait_send())

    def finish_out(i):
        bk_copy(i).wait_send()

    each(n_bk, finish_out)


def projection(fragment, acts, cot, weights, snapshot):
    tok, width = acts.shape
    rows, ffw = weights.shape
    frag = snapshot.shape[1]
    units = ffw // 2 // LANES
    chunks = units // 2
    block = 2 * rows
    pad_rows = (rows + 15) // 16 * 16
    part_rows = (pad_rows // 16 + 1) // 2 * 16
    n_x, n_bk = 3, 6
    dma = pltpu.SemaphoreType.DMA
    vmem = pltpu.VMEM
    return pl.pallas_call(
        pair_kernel,
        out_shape=(
            vmem((tok, width), bf16),
            vmem((rows, ffw), f32),
            vmem((rows, frag), f32),
        ),
        in_specs=[
            pl.BlockSpec(memory_space=pltpu.SMEM),
            pl.BlockSpec(memory_space=pl.ANY),
            pl.BlockSpec(memory_space=pl.ANY),
            pl.BlockSpec(memory_space=pl.ANY),
            pl.BlockSpec(memory_space=pl.ANY),
        ],
        out_specs=(pl.BlockSpec(memory_space=vmem),) * 3,
        scratch_shapes=[
            vmem((rows, ffw), f32),
            vmem((rows, frag), f32),
            vmem((2 * tok, width), bf16),
            vmem((2 * tok, ffw // 2), bf16),
            vmem((units, 4, 4, block, LANES), bf16),
            vmem((units, 4, 4, block, LANES), bf16),
            vmem((units, 2, 2, block, LANES), bf16),
            vmem((units, 2, 4, block, LANES), bf16),
            vmem((units, block, LANES), bf16),
            vmem((units, 2, block, LANES), bf16),
            vmem((chunks, block, LANES), bf16),
            vmem((chunks, block, LANES), bf16),
            vmem((chunks, block, LANES), bf16),
            vmem((chunks, block, LANES), bf16),
            vmem((n_bk, tok // (n_bk // 2), width // 2), bf16),
            vmem((n_bk, tok // (n_bk // 2), width // 2), bf16),
            vmem((block, LANES), f32),
            vmem((2, tok, width // 2), f32),
            vmem((block, LANES), f32),
            vmem((2, pad_rows, frag), bf16),
            vmem((pad_rows, frag), bf16),
            vmem((part_rows, frag), bf16),
            vmem((part_rows, frag), f32),
            vmem((part_rows, frag), f32),
            dma((chunks + 4,)),
            dma((units, 8)), dma((units, 8)),
            dma((units, 8)), dma((units, 8)),
            dma((chunks,)), dma((chunks,)),
            dma((n_x,)), dma((n_x,)),
            dma((chunks,)), dma((chunks,)),
            dma((n_bk,)), dma((n_bk,)),
            dma((chunks,)), dma((chunks,)),
            dma((3,)), dma((3,)),
        ],
        compiler_params=pltpu.CompilerParams(
            collective_id=1, has_side_effects=True, vmem_limit_bytes=53 * 2**20
        ),
        cost_estimate=pl.CostEstimate(
            flops=6 * tok * width * ffw, bytes_accessed=16 * tok * width, transcendentals=tok * ffw
        ),
        name="pair_projection",
    )(fragment, acts, cot, weights, snapshot)


def update_kernel(
    frag_ref, g_ref, p_ref, m_ref, v_ref, snap_ref, mom_ref, total_ref, back_ref,
    p_out, m_out, v_out, mom_out, snap_out, back_out,
    new_p, new_m, new_v, new_mom, new_snap, wide_sem, sem,
):
    frag = snap_ref.shape[1]
    blocks = wide_sem.shape[0]
    step = p_ref.shape[0] // blocks
    pass_on = pltpu.make_async_copy(back_ref, back_out, sem.at[0])
    pass_on.start()
    outer = total_ref[...] * 0.25
    mom = outer_mu * mom_ref[...] + outer
    new_mom[...] = mom
    new_snap[...] = snap_ref[...] - outer_rate * (outer + outer_mu * mom)
    copies = [
        pass_on,
        pltpu.make_async_copy(new_mom, mom_out, sem.at[1]),
        pltpu.make_async_copy(new_snap, snap_out, sem.at[2]),
    ]
    copies[1].start()
    copies[2].start()
    cols = pl.ds(pl.multiple_of(frag_ref[0] * frag, LANES), frag)
    for b in range(blocks):
        at = pl.ds(b * step, step)
        grad = g_ref[at, :]
        weights = p_ref[at, :]
        first = beta_one * m_ref[at, :] + (1.0 - beta_one) * grad
        second = beta_two * v_ref[at, :] + (1.0 - beta_two) * grad * grad
        new_m[at, :] = first
        new_v[at, :] = second
        new_p[at, :] = weights - inner_rate * (
            first / (jnp.sqrt(second) + adam_eps) + decay_rate * weights
        )
        new_p[at, cols] = mix_rate * new_snap[at, :] + (1.0 - mix_rate) * new_p[at, cols]
        for i, (src, dst) in enumerate(((new_p, p_out), (new_m, m_out), (new_v, v_out))):
            copy = pltpu.make_async_copy(src.at[at], dst.at[at], wide_sem.at[b, i])
            copy.start()
            copies.append(copy)
    for copy in copies:
        copy.wait()


def update(fragment, grad, weights, first, second, snapshot, momentum, total, back):
    full = jax.ShapeDtypeStruct(weights.shape, f32)
    part = jax.ShapeDtypeStruct(snapshot.shape, f32)
    vmem = pl.BlockSpec(memory_space=pltpu.VMEM)
    hbm = pl.BlockSpec(memory_space=pl.ANY)
    return pl.pallas_call(
        update_kernel,
        in_specs=[pl.BlockSpec(memory_space=pltpu.SMEM)] + [vmem] * 8,
        out_specs=[hbm] * 6,
        out_shape=[full] * 3 + [part] * 2 + [jax.ShapeDtypeStruct(back.shape, back.dtype)],
        scratch_shapes=[pltpu.VMEM(weights.shape, f32)] * 3
        + [pltpu.VMEM(snapshot.shape, f32)] * 2
        + [pltpu.SemaphoreType.DMA((3, 3)), pltpu.SemaphoreType.DMA((3,))],
        compiler_params=pltpu.CompilerParams(vmem_limit_bytes=24 * 2**20),
        name="update",
    )(fragment, grad, weights, first, second, snapshot, momentum, total, back)


def body(inputs, cotangent, params, first_moment, second_moment, snapshot, momentum, fragment):
    back, grad, total = projection(fragment, inputs[0], cotangent[0], params[0], snapshot)
    stepped, first, second, new_momentum, new_snapshot, input_grad = update(
        fragment, grad, params[0], first_moment[0], second_moment[0], snapshot, momentum, total, back
    )
    return (stepped[None], first[None], second[None], input_grad[None], new_momentum, new_snapshot)


def solution(mesh):
    return jax.shard_map(
        body,
        mesh=mesh,
        in_specs=(
            P("rep", "fsdp", None),
            P("rep", "fsdp", None),
            P("rep", "fsdp", None),
            P("rep", "fsdp", None),
            P("rep", "fsdp", None),
            P("fsdp", None),
            P("fsdp", None),
            P(),
        ),
        out_specs=(
            P("rep", "fsdp", None),
            P("rep", "fsdp", None),
            P("rep", "fsdp", None),
            P("rep", "fsdp", None),
            P("fsdp", None),
            P("fsdp", None),
        ),
        check_vma=False,
    )
```

```python
import functools

import jax
import jax.numpy as jnp
from jax import lax
from jax.experimental import pallas as pl
from jax.experimental.pallas import tpu as pltpu
from jax.sharding import PartitionSpec as P

beta_one = 0.9
beta_two = 0.95
inner_rate = 0.01
adam_eps = 1e-08
decay_rate = 0.1
outer_rate = 0.7
outer_mu = 0.9
mix_rate = 0.5

LANES = 128
CHUNK = 256
MESH = pl.DeviceIdType.MESH
f32 = jnp.float32
bf16 = jnp.bfloat16


def gelu_slope(t):
    c = 0.7978845608028654
    sq = t * t
    th = jnp.tanh(c * t * (1.0 + 0.044715 * sq))
    return 0.5 * (1.0 + th) + 0.5 * t * (1.0 - th * th) * (c * (1.0 + 3 * 0.044715 * sq))


def pair_kernel(
    frag_ref, x_hbm, cot_hbm, p_hbm, snap_hbm,
    out_ref, g_ref, total_ref,
    p_ref, snap_ref,
    xb, cb, w, g, rah, raf, rbh, rbf, pws, pwr, gps, gpr, bks, bkr, tmp, acc, pair_tmp, ds, dr, dq, dt, du,
    loc_sem, ag_send, ag_recv, rs_send, rs_recv, pw_send, pw_recv,
    x_send, x_recv, cot_send, cot_recv, bk_send, bk_recv, gp_send, gp_recv, d_send, d_recv,
):
    tok, width = x_hbm.shape
    rows, ffw = p_ref.shape
    half_cols = ffw // 2
    n_chunks = half_cols // CHUNK
    block = 2 * rows
    pad_rows = ds.shape[1]
    core = lax.rem(lax.axis_index("rep"), 2)
    frag = snap_ref.shape[1]
    cut = (block // 16 + 1) // 2 * 16
    n_x = x_send.shape[0]
    x_rows = tok // n_x
    n_bk = bk_send.shape[0]
    bk_rows = tok // (n_bk // 2)
    bk_cols = width // 2
    scale = width ** (-0.5)
    ahead = 6
    work_lag = 10
    done = work_lag + n_chunks

    f = lax.axis_index("fsdp")
    r = lax.axis_index("rep")
    yh = lax.rem(f, 2)
    x = lax.rem(lax.div(f, 2), 4)
    z = lax.div(f, 8)

    def device(zz, xx, yy):
        return {"fsdp": zz * 8 + xx * 2 + yy}

    peer = device(z, x, 1 - yh)
    sibling = {"rep": r + 1 - 2 * lax.rem(r, 2)}
    neighbour = {"rep": lax.rem(r + 2, 4)}
    place = {"x": x, "z": z}
    after = {a: lax.rem(place[a] + 1, 4) for a in place}
    before = {a: lax.rem(place[a] + 3, 4) for a in place}
    across = {a: lax.rem(place[a] + 2, 4) for a in place}
    right = {"x": device(z, after["x"], yh), "z": device(after["z"], x, yh)}
    left = {"x": device(z, before["x"], yh), "z": device(before["z"], x, yh)}
    first_axis = ("x", "z")
    second_axis = ("z", "x")
    my_base = yh * half_cols
    peer_base = (1 - yh) * half_cols

    def seg2(ref, u, p, i):
        return ref.at[u, i] if p == 0 else ref.at[u, :, i]

    def half2(ref, u, p, i, h):
        part = pl.ds(2 * h, 2)
        return ref.at[u, i, part] if p == 0 else ref.at[u, part, i]

    def seg1(ref, u, p, i):
        return ref.at[u, z, i] if p == 0 else ref.at[u, i, x]

    def half1(ref, u, p, i, h):
        part = pl.ds(0, cut) if h == 0 else pl.ds(cut, block - cut)
        return ref.at[u, z, i, part] if p == 0 else ref.at[u, i, x, part]

    def chunk_cols(c):
        return pl.ds(pl.multiple_of(c * CHUNK, CHUNK), CHUNK)

    def remote(src, dst, send, recv, to):
        return pltpu.make_async_remote_copy(
            src_ref=src, dst_ref=dst, send_sem=send, recv_sem=recv, device_id=to, device_id_type=MESH
        )

    def gather_copy(u, p, k):
        a, b = first_axis[p], second_axis[p]
        part = (
            lambda: seg1(w, u, p, place[a]),
            lambda: seg1(w, u, p, place[a]),
            lambda: half1(w, u, p, before[a], 0),
            lambda: half1(w, u, p, after[a], 1),
            lambda: seg2(w, u, p, place[b]),
            lambda: seg2(w, u, p, place[b]),
            lambda: half2(w, u, p, before[b], 0),
            lambda: half2(w, u, p, after[b], 1),
        )[k]()
        to = (right if k % 2 == 0 else left)[a if k < 4 else b]
        return remote(part, part, ag_send.at[u, k], ag_recv.at[u, k], to)

    def scatter_copy(u, p, k):
        a, b = first_axis[p], second_axis[p]
        src, dst = (
            lambda: (half2(g, u, p, across[b], 0), rah.at[u, 0]),
            lambda: (half2(g, u, p, across[b], 1), rah.at[u, 1]),
            lambda: (seg2(g, u, p, after[b]), raf.at[u, 0]),
            lambda: (seg2(g, u, p, before[b]), raf.at[u, 1]),
            lambda: (half1(g, u, p, across[a], 0), rbh.at[u, pl.ds(0, cut)]),
            lambda: (half1(g, u, p, across[a], 1), rbh.at[u, pl.ds(cut, block - cut)]),
            lambda: (seg1(g, u, p, after[a]), rbf.at[u, 0]),
            lambda: (seg1(g, u, p, before[a]), rbf.at[u, 1]),
        )[k]()
        to = (right if k % 2 == 0 else left)[b if k < 4 else a]
        return remote(src, dst, rs_send.at[u, k], rs_recv.at[u, k], to)

    def pw_copy(c):
        return remote(pws.at[c], pwr.at[c], pw_send.at[c], pw_recv.at[c], peer)

    def x_copy(i):
        return remote(
            x_hbm.at[pl.ds(i * x_rows, x_rows)], xb.at[pl.ds(tok + i * x_rows, x_rows)],
            x_send.at[i], x_recv.at[i], peer,
        )

    def cot_copy(c):
        cols = pl.ds(pl.multiple_of(peer_base + c * CHUNK, CHUNK), CHUNK)
        return remote(
            cot_hbm.at[:, cols], cb.at[pl.ds(tok, tok), chunk_cols(c)],
            cot_send.at[c], cot_recv.at[c], peer,
        )

    def bk_copy(i):
        return remote(bks.at[i], bkr.at[i], bk_send.at[i], bk_recv.at[i], peer)

    def gp_copy(c):
        return remote(gps.at[c], gpr.at[c], gp_send.at[c], gp_recv.at[c], peer)

    def d_copy(i):
        src, dst, to = (
            (ds.at[0], dr, sibling),
            (dt, du, sibling),
        )[i]
        return remote(src, dst, d_send.at[i], d_recv.at[i], to)

    def on_second(step):
        pl.when(core == 1)(step)

    def across_y():
        return remote(ds.at[1], dq, d_send.at[2], d_recv.at[2], neighbour)

    def add_chips():
        across_y().wait_recv()
        dt[...] = ds[1].astype(f32) + dq[...].astype(f32)
        d_copy(1).start()

    def own_x():
        return pltpu.make_async_copy(x_hbm, xb.at[pl.ds(0, tok)], loc_sem.at[n_chunks])

    def own_params(h):
        cols = pl.ds(pl.multiple_of((my_base, peer_base)[h], LANES), half_cols)
        return pltpu.make_async_copy(p_hbm.at[:, cols], p_ref.at[:, cols], loc_sem.at[n_chunks + 2 + h])

    def own_snap():
        return pltpu.make_async_copy(snap_hbm, snap_ref, loc_sem.at[n_chunks + 1])

    def own_cot(c):
        cols = pl.ds(pl.multiple_of(my_base + c * CHUNK, CHUNK), CHUNK)
        return pltpu.make_async_copy(
            cot_hbm.at[:, cols], cb.at[pl.ds(0, tok), chunk_cols(c)], loc_sem.at[c]
        )

    def each(count, step):
        def run(i, carry):
            step(i)
            return carry
        lax.fori_loop(0, count, run, 0)

    def ranged(t, lag, step):
        @pl.when((t >= lag) & (t < lag + n_chunks))
        def _():
            step(t - lag)

    def both(step):
        def run(c):
            for p in range(2):
                step(2 * c + p, p)
        return run

    barrier = pltpu.get_barrier_semaphore()
    partners = (peer, right["x"], left["x"], right["z"], left["z"], sibling, neighbour)
    for partner in partners:
        pl.semaphore_signal(barrier, inc=1, device_id=partner, device_id_type=MESH)
    own_params(1).start()
    own_params(0).start()
    own_snap().start()
    own_params(1).wait()
    pl.semaphore_wait(barrier, len(partners))

    def prepare(c):
        parts = []
        for h in range(2):
            cols = pl.ds(pl.multiple_of(peer_base + c * CHUNK + h * LANES, LANES), LANES)
            parts.append(p_ref[:, cols])
        pws[c] = jnp.concatenate(parts, axis=0).astype(bf16)
        pw_copy(c).start()

    each(n_chunks, prepare)
    each(n_x, lambda i: x_copy(i).start())
    own_x().start()
    each(n_chunks, lambda c: own_cot(c).start())
    own_snap().wait()
    own_params(0).wait()
    local = p_ref[:, :frag]
    for i in range(1, ffw // frag):
        local = jnp.where(frag_ref[0] == i, p_ref[:, i * frag : (i + 1) * frag], local)
    delta = snap_ref[...] - local
    ds[0] = jnp.concatenate([delta, jnp.zeros((pad_rows - rows, frag), f32)], axis=0).astype(bf16)

    d_copy(0).start()

    def chunk_weights(c):
        return jnp.concatenate(
            [w[2 * c].reshape(width, LANES), w[2 * c + 1].reshape(width, LANES)], axis=1
        )

    def hidden(c, start):
        at = pl.ds(start, tok)
        pre = jnp.dot(xb[at, :], chunk_weights(c), preferred_element_type=f32) * scale
        cot = cb[at, chunk_cols(c)].astype(f32)
        cb[at, chunk_cols(c)] = (gelu_slope(pre) * cot * scale).astype(bf16)

    def gather_own(c):
        pw_copy(c).wait_recv()
        pair_tmp[...] = pwr[c].astype(f32)
        for h in range(2):
            cols = pl.ds(pl.multiple_of(my_base + c * CHUNK + h * LANES, LANES), LANES)
            tmp[pl.ds(pl.multiple_of(yh * rows, 8), rows), :] = p_ref[:, cols]
            tmp[pl.ds(pl.multiple_of((1 - yh) * rows, 8), rows), :] = pair_tmp[pl.ds(h * rows, rows), :]
            w[2 * c + h, z, x] = tmp[...].astype(bf16)
            gather_copy(2 * c + h, h, 0).start()
            gather_copy(2 * c + h, h, 1).start()

    def gather_forward(k):
        def step(u, p):
            gather_copy(u, p, k).wait_recv()
            gather_copy(u, p, k + 2).start()
            gather_copy(u, p, k + 1).wait_recv()
            gather_copy(u, p, k + 3).start()
        return both(step)

    @both
    def gather_second(u, p):
        gather_copy(u, p, 2).wait_recv()
        gather_copy(u, p, 3).wait_recv()
        gather_copy(u, p, 4).start()
        gather_copy(u, p, 5).start()

    @both
    def gather_end(u, p):
        gather_copy(u, p, 6).wait_recv()
        gather_copy(u, p, 7).wait_recv()

    def own_hidden(c):
        gather_end(c)
        own_cot(c).wait()
        hidden(c, 0)

    def add_into(ref, other):
        ref[...] = (ref[...].astype(f32) + other[...].astype(f32)).astype(bf16)

    def back_part(n, start, units):
        part = jnp.concatenate(
            [w[u, pl.ds(2 * n, 2)].reshape(bk_cols, LANES) for u in units], axis=1
        )
        cols = slice(units[0] * LANES, (units[-1] + 1) * LANES)
        return lax.dot_general(
            cb[pl.ds(start, tok), cols], part, (((1,), (1,)), ((), ())), preferred_element_type=f32
        )

    def send_back(n, term):
        for m in range(n_bk // 2):
            i = n * (n_bk // 2) + m
            bks[i] = term[m * bk_rows : (m + 1) * bk_rows].astype(bf16)
            bk_copy(i).start()

    middle = n_chunks // 2
    early = range(2 * middle)
    late = range(2 * middle, 2 * n_chunks - 2)
    final = range(2 * n_chunks - 2, 2 * n_chunks)

    def work(c):
        @pl.when(c == middle)
        def _():
            acc[0] = back_part(0, tok, early)

        @pl.when(c == n_chunks - 1)
        def _():
            on_second(lambda: across_y().start())
            acc[0] = acc[0] + back_part(0, tok, late)

        cot_copy(c).wait_recv()

        @pl.when(c + ahead < n_chunks)
        def _():
            cot_copy(c + ahead).start()

        hidden(c, tok)

        @pl.when(c == n_chunks - 1)
        def _():
            send_back(0, acc[0] + back_part(0, tok, final))

        term = lax.dot_general(
            xb[...], cb[:, chunk_cols(c)], (((0,), (0,)), ((), ())), preferred_element_type=f32
        ).astype(bf16)
        for h in range(2):
            g[2 * c + h] = term[:, h * LANES : (h + 1) * LANES].reshape(4, 4, block, LANES)
        for p in range(2):
            scatter_copy(2 * c + p, p, 0).start()
            scatter_copy(2 * c + p, p, 1).start()

    @both
    def scatter_second(u, p):
        b = second_axis[p]
        scatter_copy(u, p, 0).wait_recv()
        add_into(half2(g, u, p, after[b], 0), rah.at[u, 0])
        scatter_copy(u, p, 2).start()
        scatter_copy(u, p, 1).wait_recv()
        add_into(half2(g, u, p, before[b], 1), rah.at[u, 1])
        scatter_copy(u, p, 3).start()

    @both
    def scatter_third(u, p):
        b = second_axis[p]
        scatter_copy(u, p, 2).wait_recv()
        scatter_copy(u, p, 3).wait_recv()
        mine = seg2(g, u, p, place[b])
        mine[...] = (
            mine[...].astype(f32) + raf[u, 0].astype(f32) + raf[u, 1].astype(f32)
        ).astype(bf16)
        scatter_copy(u, p, 4).start()
        scatter_copy(u, p, 5).start()

    @both
    def scatter_fourth(u, p):
        a = first_axis[p]
        scatter_copy(u, p, 4).wait_recv()
        add_into(half1(g, u, p, after[a], 0), rbh.at[u, pl.ds(0, cut)])
        scatter_copy(u, p, 6).start()
        scatter_copy(u, p, 5).wait_recv()
        add_into(half1(g, u, p, before[a], 1), rbh.at[u, pl.ds(cut, block - cut)])
        scatter_copy(u, p, 7).start()

    @both
    def scatter_end(u, p):
        a = first_axis[p]
        for k in range(6):
            scatter_copy(u, p, k).wait_send()
        scatter_copy(u, p, 6).wait_recv()
        scatter_copy(u, p, 7).wait_recv()
        mine = seg1(g, u, p, place[a])
        tmp[...] = mine[...].astype(f32) + rbf[u, 0].astype(f32) + rbf[u, 1].astype(f32)
        pair_tmp[pl.ds(p * rows, rows), :] = tmp[pl.ds(pl.multiple_of((1 - yh) * rows, 8), rows), :]
        cols = pl.ds(pl.multiple_of(my_base + u * LANES, LANES), LANES)
        g_ref[:, cols] = tmp[pl.ds(pl.multiple_of(yh * rows, 8), rows), :]
        if p == 1:
            c = lax.div(u, 2)
            gps[c] = pair_tmp[...].astype(bf16)
            gp_copy(c).start()

    def keep_back(n):
        acc[n] = back_part(n, 0, range(2 * n_chunks))

    def settle(c):
        pw_copy(c).wait_send()
        cot_copy(c).wait_send()
        for p in range(2):
            for k in range(8):
                gather_copy(2 * c + p, p, k).wait_send()

    def tick(t):
        ranged(t, 0, gather_own)
        ranged(t, 1, gather_forward(0))
        ranged(t, 2, gather_second)
        ranged(t, 3, gather_forward(4))

        @pl.when(t == 4)
        def _():
            own_x().wait()

        ranged(t, 4, own_hidden)

        @pl.when(t == 1)
        def _():
            d_copy(0).wait_recv()
            ds[1] = (ds[0].astype(f32) + dr[...].astype(f32)).astype(bf16)

        @pl.when(t == 8)
        def _():
            for c in range(ahead):
                cot_copy(c).start()

        @pl.when(t == work_lag)
        def _():
            for i in range(n_x):
                x_copy(i).wait_recv()

        ranged(t, work_lag, work)

        @pl.when(t == done)
        def _():
            send_back(1, back_part(1, tok, range(2 * n_chunks)))

        @pl.when((t >= done + 1) & (t < done + 3))
        def _():
            keep_back(t - done - 1)

        ranged(t, work_lag + 2, settle)
        ranged(t, work_lag + 3, scatter_second)
        ranged(t, work_lag + 6, scatter_third)
        ranged(t, work_lag + 8, scatter_fourth)
        ranged(t, work_lag + 9, scatter_end)

    each(n_chunks + work_lag + 9, tick)

    def finish_back(i):
        bk_copy(i).wait_recv()
        n, m = lax.div(i, n_bk // 2), lax.rem(i, n_bk // 2)
        at = pl.ds(pl.multiple_of(m * bk_rows, 16), bk_rows)
        cols = pl.ds(pl.multiple_of(n * bk_cols, LANES), bk_cols)
        out_ref[at, cols] = (acc[n, at, :] + bkr[i].astype(f32)).astype(bf16)


    def finish_grad(c):
        gp_copy(c).wait_recv()
        pair_tmp[...] = gpr[c].astype(f32)
        for h in range(2):
            cols = pl.ds(pl.multiple_of(peer_base + c * CHUNK + h * LANES, LANES), LANES)
            g_ref[:, cols] = pair_tmp[pl.ds(h * rows, rows), :]

    on_second(add_chips)
    each(n_bk, finish_back)

    @pl.when(core == 0)
    def _():
        d_copy(1).wait_recv()
        total_ref[...] = du[...][:rows]

    @pl.when(core == 1)
    def _():
        total_ref[...] = dt[...][:rows]

    each(n_chunks, finish_grad)

    def finish(c):
        gp_copy(c).wait_send()
        for p in range(2):
            for k in range(6, 8):
                scatter_copy(2 * c + p, p, k).wait_send()

    each(n_chunks, finish)
    each(n_x, lambda i: x_copy(i).wait_send())
    d_copy(0).wait_send()
    on_second(lambda: d_copy(1).wait_send())
    on_second(lambda: across_y().wait_send())

    def finish_out(i):
        bk_copy(i).wait_send()

    each(n_bk, finish_out)


def projection(fragment, acts, cot, weights, snapshot):
    tok, width = acts.shape
    rows, ffw = weights.shape
    frag = snapshot.shape[1]
    units = ffw // 2 // LANES
    chunks = units // 2
    block = 2 * rows
    pad_rows = (rows + 15) // 16 * 16
    n_x, n_bk = 3, 6
    dma = pltpu.SemaphoreType.DMA
    vmem = pltpu.VMEM
    return pl.pallas_call(
        pair_kernel,
        out_shape=(
            vmem((tok, width), bf16),
            vmem((rows, ffw), f32),
            vmem((rows, frag), f32),
        ),
        in_specs=[
            pl.BlockSpec(memory_space=pltpu.SMEM),
            pl.BlockSpec(memory_space=pl.ANY),
            pl.BlockSpec(memory_space=pl.ANY),
            pl.BlockSpec(memory_space=pl.ANY),
            pl.BlockSpec(memory_space=pl.ANY),
        ],
        out_specs=(pl.BlockSpec(memory_space=vmem),) * 3,
        scratch_shapes=[
            vmem((rows, ffw), f32),
            vmem((rows, frag), f32),
            vmem((2 * tok, width), bf16),
            vmem((2 * tok, ffw // 2), bf16),
            vmem((units, 4, 4, block, LANES), bf16),
            vmem((units, 4, 4, block, LANES), bf16),
            vmem((units, 2, 2, block, LANES), bf16),
            vmem((units, 2, 4, block, LANES), bf16),
            vmem((units, block, LANES), bf16),
            vmem((units, 2, block, LANES), bf16),
            vmem((chunks, block, LANES), bf16),
            vmem((chunks, block, LANES), bf16),
            vmem((chunks, block, LANES), bf16),
            vmem((chunks, block, LANES), bf16),
            vmem((n_bk, tok // (n_bk // 2), width // 2), bf16),
            vmem((n_bk, tok // (n_bk // 2), width // 2), bf16),
            vmem((block, LANES), f32),
            vmem((2, tok, width // 2), f32),
            vmem((block, LANES), f32),
            vmem((2, pad_rows, frag), bf16),
            vmem((pad_rows, frag), bf16),
            vmem((pad_rows, frag), bf16),
            vmem((pad_rows, frag), f32),
            vmem((pad_rows, frag), f32),
            dma((chunks + 4,)),
            dma((units, 8)), dma((units, 8)),
            dma((units, 8)), dma((units, 8)),
            dma((chunks,)), dma((chunks,)),
            dma((n_x,)), dma((n_x,)),
            dma((chunks,)), dma((chunks,)),
            dma((n_bk,)), dma((n_bk,)),
            dma((chunks,)), dma((chunks,)),
            dma((3,)), dma((3,)),
        ],
        compiler_params=pltpu.CompilerParams(
            collective_id=1, has_side_effects=True, vmem_limit_bytes=53 * 2**20
        ),
        cost_estimate=pl.CostEstimate(
            flops=6 * tok * width * ffw, bytes_accessed=16 * tok * width, transcendentals=tok * ffw
        ),
        name="pair_projection",
    )(fragment, acts, cot, weights, snapshot)


def update_kernel(
    frag_ref, g_ref, p_ref, m_ref, v_ref, snap_ref, mom_ref, total_ref, back_ref,
    p_out, m_out, v_out, mom_out, snap_out, back_out,
    new_p, new_m, new_v, new_mom, new_snap, wide_sem, sem,
):
    frag = snap_ref.shape[1]
    blocks = wide_sem.shape[0]
    step = p_ref.shape[0] // blocks
    pass_on = pltpu.make_async_copy(back_ref, back_out, sem.at[0])
    pass_on.start()
    outer = total_ref[...] * 0.25
    mom = outer_mu * mom_ref[...] + outer
    new_mom[...] = mom
    new_snap[...] = snap_ref[...] - outer_rate * (outer + outer_mu * mom)
    copies = [
        pass_on,
        pltpu.make_async_copy(new_mom, mom_out, sem.at[1]),
        pltpu.make_async_copy(new_snap, snap_out, sem.at[2]),
    ]
    copies[1].start()
    copies[2].start()
    cols = pl.ds(pl.multiple_of(frag_ref[0] * frag, LANES), frag)
    for b in range(blocks):
        at = pl.ds(b * step, step)
        grad = g_ref[at, :]
        weights = p_ref[at, :]
        first = beta_one * m_ref[at, :] + (1.0 - beta_one) * grad
        second = beta_two * v_ref[at, :] + (1.0 - beta_two) * grad * grad
        new_m[at, :] = first
        new_v[at, :] = second
        new_p[at, :] = weights - inner_rate * (
            first / (jnp.sqrt(second) + adam_eps) + decay_rate * weights
        )
        new_p[at, cols] = mix_rate * new_snap[at, :] + (1.0 - mix_rate) * new_p[at, cols]
        for i, (src, dst) in enumerate(((new_p, p_out), (new_m, m_out), (new_v, v_out))):
            copy = pltpu.make_async_copy(src.at[at], dst.at[at], wide_sem.at[b, i])
            copy.start()
            copies.append(copy)
    for copy in copies:
        copy.wait()


def update(fragment, grad, weights, first, second, snapshot, momentum, total, back):
    full = jax.ShapeDtypeStruct(weights.shape, f32)
    part = jax.ShapeDtypeStruct(snapshot.shape, f32)
    vmem = pl.BlockSpec(memory_space=pltpu.VMEM)
    hbm = pl.BlockSpec(memory_space=pl.ANY)
    return pl.pallas_call(
        update_kernel,
        in_specs=[pl.BlockSpec(memory_space=pltpu.SMEM)] + [vmem] * 8,
        out_specs=[hbm] * 6,
        out_shape=[full] * 3 + [part] * 2 + [jax.ShapeDtypeStruct(back.shape, back.dtype)],
        scratch_shapes=[pltpu.VMEM(weights.shape, f32)] * 3
        + [pltpu.VMEM(snapshot.shape, f32)] * 2
        + [pltpu.SemaphoreType.DMA((3, 3)), pltpu.SemaphoreType.DMA((3,))],
        compiler_params=pltpu.CompilerParams(vmem_limit_bytes=24 * 2**20),
        name="update",
    )(fragment, grad, weights, first, second, snapshot, momentum, total, back)


def body(inputs, cotangent, params, first_moment, second_moment, snapshot, momentum, fragment):
    back, grad, total = projection(fragment, inputs[0], cotangent[0], params[0], snapshot)
    stepped, first, second, new_momentum, new_snapshot, input_grad = update(
        fragment, grad, params[0], first_moment[0], second_moment[0], snapshot, momentum, total, back
    )
    return (stepped[None], first[None], second[None], input_grad[None], new_momentum, new_snapshot)


def solution(mesh):
    return jax.shard_map(
        body,
        mesh=mesh,
        in_specs=(
            P("rep", "fsdp", None),
            P("rep", "fsdp", None),
            P("rep", "fsdp", None),
            P("rep", "fsdp", None),
            P("rep", "fsdp", None),
            P("fsdp", None),
            P("fsdp", None),
            P(),
        ),
        out_specs=(
            P("rep", "fsdp", None),
            P("rep", "fsdp", None),
            P("rep", "fsdp", None),
            P("rep", "fsdp", None),
            P("fsdp", None),
            P("fsdp", None),
        ),
        check_vma=False,
    )
```
